512 devices in a mesh: grp: 8 (over z), dom: 64 (over x, y, core).
Axes of the slice: x: 4, y: 8, z: 8, core: 2. Of those that a mesh axis runs over, the one named last changes fastest.
Arguments:
- features: bfloat16 [65536, 512], P(('grp', 'dom')), may hold values from -6 to 6
- w_self: bfloat16 [512, 512], replicated, may hold values from -0.25 to 0.25
- w_neigh: bfloat16 [512, 512], replicated, may hold values from -1 to 1
- cotangent: bfloat16 [65536, 512], P(('grp', 'dom')), may hold values from -6 to 6
- neighbors: int32 [65536, 16], P(('grp', 'dom')), may hold values from 0 to 639, as said below
- send_rows: int32 [8, 64, 64, 8], P('grp', 'dom'), may hold values from 0 to 127, as said below
- send_count: int32 [8, 64, 64], P('grp', 'dom'), may hold values from 1 to 8, as said below
Outputs:
- grad_features: bfloat16 [65536, 512], P(('grp', 'dom'))
- grad_w_self: float32 [512, 512], replicated
- grad_w_neigh: float32 [512, 512], replicated
The draws below stay inside these ranges and needn't reach their ends.
Inputs may be any that keep to these rules, and one draw needn't show every extreme that they name: `send_rows`: within one (g, p, d) the 8 slots name distinct rows. `send_count`: every partition receives the full 8 from at least one sender of its group. `neighbors`: in each row the first 8 entries name own rows of the node's partition; the others are 128 + p * 8 + s, a live slot s of peer p's boundary rows to that partition.
All inputs are finite; a program needn't handle non-finite values.
Results may differ from the reference program's by a relative error of at most 0.0063.
Values may be sent and summed in bfloat16 or wider, within the bound.
A program may use at most 64 MiB of HBM per device.

```python
import jax
import jax.numpy as jnp
from jax import lax

D = 512
NODES_DEV = 128
BMAX = 8
DEG = 16
NODES = 65536
N_GRP = 8
N_DOM = 64


def boundary_counts(key):
    key = jax.random.fold_in(key, 101)
    first_key, second_key = jax.random.split(key)
    counts = jax.random.randint(first_key, (N_GRP, N_DOM, N_DOM), 1, BMAX + 1)
    offset = jax.random.randint(second_key, (N_GRP, 1, N_DOM), 0, N_DOM)
    sender = (jnp.arange(N_DOM, dtype=jnp.int32)[None, None, :] + offset) % N_DOM
    full_pair = jnp.arange(N_DOM, dtype=jnp.int32)[None, :, None] == sender
    return jnp.where(full_pair, BMAX, counts).astype(jnp.int32)


def draw_send_count(key, part):
    return boundary_counts(key)


def draw_send_rows(key, part):
    key = jax.random.fold_in(key, 7)
    total = N_GRP * N_DOM * N_DOM
    scores = jax.random.randint(key, (total, NODES_DEV), 0, 2 ** 30 // NODES_DEV) * NODES_DEV + jnp.arange(NODES_DEV, dtype=jnp.int32)[None, :]
    order = jnp.argsort(scores, axis=1, stable=True)[:, :BMAX]
    return order.reshape(N_GRP, N_DOM, N_DOM, BMAX).astype(jnp.int32)


def draw_neighbors(key, part):
    counts = boundary_counts(key)
    key = jax.random.fold_in(key, 13)
    own_key, order_key, slot_key = jax.random.split(key, 3)
    device_count = N_GRP * N_DOM
    half_degree = DEG // 2
    spread = NODES_DEV * half_degree
    own_part = jax.random.randint(own_key, (device_count, NODES_DEV, half_degree), 0, NODES_DEV)
    scores = jax.random.randint(order_key, (device_count, spread), 0, 2 ** 30 // spread) * spread + jnp.arange(spread, dtype=jnp.int32)[None, :]
    order = jnp.argsort(scores, axis=1, stable=True).astype(jnp.int32)
    peer = order % N_DOM
    received = jnp.transpose(counts, (0, 2, 1)).reshape(device_count, N_DOM)
    limit = jnp.take_along_axis(received, peer, axis=1)
    slot = jax.random.randint(slot_key, (device_count, spread), 0, limit)
    halo_part = (NODES_DEV + peer * BMAX + slot).reshape(device_count, NODES_DEV, half_degree)
    return jnp.concatenate([own_part, halo_part], axis=2).reshape(device_count * NODES_DEV, DEG).astype(jnp.int32)


def shard_levels(key, dims, cuts, low, largest):
    factor_of, own = 1.0, jax.random.fold_in(key, 6)
    for dim, shards_of in cuts:
        draws = jnp.exp(jax.random.uniform(jax.random.fold_in(own, dim), (shards_of,), jnp.float32, low / len(cuts), largest / len(cuts)))
        factor_of = factor_of * jnp.repeat(draws, dims[dim] // shards_of).reshape([-1 if axis == dim else 1 for axis in range(len(dims))])
    return factor_of


def gaussian(key, shape, width, most, pieces=(), held_as=jnp.bfloat16):
    values = jax.random.normal(key, shape, jnp.float32) * width
    if len(pieces) > 0:
        values = shard_levels(key, shape, pieces, -0.22, 0.18) * values
    return jnp.clip(values, min=-most, max=most).astype(held_as)


def setup_inputs(seed: int = 0) -> dict:
    keys = jax.random.split(jax.random.key(seed), 8)
    return {
        "features": gaussian(keys[0], (NODES, D), 1.0, 6.0, ((0, 512),)),
        "w_self": gaussian(keys[1], (D, D), D ** -0.5, 0.25),
        "w_neigh": gaussian(keys[2], (D, D), (D // DEG) ** -0.5, 1.0),
        "cotangent": gaussian(keys[3], (NODES, D), 1.0, 6.0, ((0, 512),)),
        "neighbors": draw_neighbors(jax.random.fold_in(keys[7], 71), 0),
        "send_rows": draw_send_rows(jax.random.fold_in(keys[7], 71), 0),
        "send_count": draw_send_count(jax.random.fold_in(keys[7], 71), 0),
    }


def reference(features, w_self, w_neigh, cotangent, neighbors, send_rows, send_count):
    device_count = N_GRP * N_DOM
    halo_width = N_DOM * BMAX
    device_ids = jnp.arange(device_count, dtype=jnp.int32)
    group_ids = device_ids // N_DOM
    member_ids = device_ids % N_DOM
    peer_ids = jnp.arange(N_DOM, dtype=jnp.int32)
    halo_rows = send_rows[group_ids[:, None], peer_ids[None, :], member_ids[:, None]]
    halo_count = send_count[group_ids[:, None], peer_ids[None, :], member_ids[:, None]]
    halo_source = ((group_ids[:, None, None] * N_DOM + peer_ids[None, :, None]) * NODES_DEV + halo_rows).reshape(device_count, halo_width).astype(jnp.int32)
    halo_live = (jnp.arange(BMAX, dtype=jnp.int32)[None, None, :] < halo_count[:, :, None]).reshape(device_count, halo_width)
    own_source = device_ids[:, None] * NODES_DEV + jnp.arange(NODES_DEV, dtype=jnp.int32)[None, :]
    ext_source = jnp.concatenate([own_source, halo_source], axis=1)
    ext_live = jnp.concatenate([jnp.ones((device_count, NODES_DEV), dtype=bool), halo_live], axis=1)
    node_device = jnp.arange(NODES, dtype=jnp.int32) // NODES_DEV
    sources = ext_source[node_device[:, None], neighbors]
    live_refs = ext_live[node_device[:, None], neighbors]
    rows_wide = features.astype(jnp.float32)
    summed = jnp.zeros((NODES, D), jnp.float32)
    for column in range(DEG):
        summed = summed + jnp.where(live_refs[:, column, None], rows_wide[sources[:, column]], jnp.float32(0.0))
    aggregate = (summed / DEG).astype(jnp.bfloat16)
    pre_act = jnp.dot(features, w_self, preferred_element_type=jnp.float32) + jnp.dot(aggregate, w_neigh, preferred_element_type=jnp.float32)
    _, backward = jax.vjp(jax.nn.gelu, pre_act)
    grad_pre = backward(cotangent.astype(pre_act.dtype))[0].astype(jnp.bfloat16)
    grad_scale = float(NODES) ** (-0.5)
    grad_w_self = jnp.dot(features.T, grad_pre, preferred_element_type=jnp.float32) * grad_scale
    grad_w_neigh = jnp.dot(aggregate.T, grad_pre, preferred_element_type=jnp.float32) * grad_scale
    grad_agg = (jnp.dot(grad_pre, w_neigh.T, preferred_element_type=jnp.float32) / DEG).astype(jnp.bfloat16)
    agg_wide = grad_agg.astype(jnp.float32)
    grad_rows = jnp.dot(grad_pre, w_self.T, preferred_element_type=jnp.float32)
    halo_total = device_count * halo_width
    halo_grad = jnp.zeros((halo_total, D), jnp.float32)
    for column in range(DEG):
        entries = neighbors[:, column]
        own_entry = entries < NODES_DEV
        grad_rows = grad_rows.at[jnp.where(own_entry, sources[:, column], NODES)].add(agg_wide, mode='drop')
        slot_ids = node_device * halo_width + entries - NODES_DEV
        halo_grad = halo_grad.at[jnp.where(own_entry, halo_total, slot_ids)].add(agg_wide, mode='drop')
    halo_back = lax.optimization_barrier(halo_grad.astype(jnp.bfloat16)).astype(jnp.float32)
    targets = jnp.where(halo_live, halo_source, NODES).reshape(-1)
    grad_rows = grad_rows.at[targets].add(halo_back, mode='drop')
    return (grad_rows.astype(jnp.bfloat16), grad_w_self, grad_w_neigh)
```

```python
import functools

import jax
import jax.numpy as jnp
from jax import lax
from jax.experimental import pallas as pl
from jax.experimental.pallas import tpu as pltpu
from jax.sharding import PartitionSpec as P

MESH = pl.DeviceIdType.MESH
F32 = jnp.float32
BF16 = jnp.bfloat16


def dot(left, right, left_dim=1, right_dim=0):
    return lax.dot_general(
        left, right, (((left_dim,), (right_dim,)), ((), ())), preferred_element_type=F32
    )


def iota(shape, dim):
    return lax.broadcasted_iota(jnp.int32, shape, dim)


def gelu_slope(v):
    root = 0.7978845608028654
    square = v * v
    t = jnp.tanh(root * (v + 0.044715 * square * v))
    return 0.5 * (1.0 + t) + (0.5 * root) * v * (1.0 - t * t) * (1.0 + 0.134145 * square)


def kernel(
    feat_ref, ws_ref, wn_ref, cot_ref, nb_ref, rows_ref, count_ref,
    gfeat_ref, gw_ref,
    sel_ref, adj_ref, adjt_ref, out_ref, halo_ref, back_ref, ret_ref,
    lt_ref, own_ref, pair_out, pair_in, z_out, z_in, xy_out, xy_in, ag_ref, agz_ref, full_ref, base_ref,
    a2a_send, a2a_recv, pair_send, pair_recv, z_send, z_recv, xy_send, xy_recv,
    ag1_send, ag1_recv, ag2_send, ag2_recv, fin_send, fin_recv,
):
    grp = lax.axis_index("grp")
    dom = lax.axis_index("dom")
    core = lax.rem(dom, 2)
    place = dom // 2
    other = 1 - core
    sibling = dom + 1 - 2 * core

    def dom_peer(r):
        return lax.rem(dom + r, 64)

    def grp_peer(r):
        return lax.rem(grp + r, 8)

    def place_peer(r):
        return lax.rem(place + r, 32)

    def loop(first, last, body):
        lax.fori_loop(first, last, lambda i, c: (body(i), c)[1], 0)

    def remote(src, dst, send, recv, device):
        return pltpu.make_async_remote_copy(
            src_ref=src, dst_ref=dst, send_sem=send, recv_sem=recv,
            device_id=device, device_id_type=MESH,
        )

    def wait(ref, sem):
        pltpu.make_async_copy(ref, ref, sem).wait()

    barrier = pltpu.get_barrier_semaphore()
    loop(1, 64, lambda r: pl.semaphore_signal(
        barrier, inc=1, device_id={"dom": dom_peer(r)}, device_id_type=MESH))
    loop(1, 8, lambda r: pl.semaphore_signal(
        barrier, inc=1, device_id={"grp": grp_peer(r)}, device_id_type=MESH))

    col = iota((1, 1024), 1)
    slot_of = jnp.bitwise_and(col, 7)
    half_of = jnp.bitwise_and(lax.shift_right_logical(col, 3), 1)
    peer_of = lax.shift_right_logical(col, 4)
    in_peer = iota((64, 1024), 0) == peer_of
    in_slot = (iota((8, 1024), 0) == slot_of).astype(BF16)
    spread = dot(rows_ref[...].astype(F32).astype(BF16), in_slot)
    row = jnp.sum(jnp.where(in_peer, spread, 0.0), axis=0, keepdims=True)
    counts = jnp.broadcast_to(count_ref[...], (8, 64)).astype(F32).astype(BF16)
    live = dot(counts, in_peer.astype(BF16))[0:1] > slot_of.astype(F32)
    target = jnp.where(live, row + 128.0 * half_of.astype(F32), 512.0)
    sel_ref[...] = (iota((256, 1024), 0).astype(F32) == target).astype(BF16)
    feat = feat_ref[...]
    feat2 = jnp.concatenate([feat[:, :256], feat[:, 256:]], axis=0)
    out_ref[...] = dot(sel_ref[...], feat2, 0, 0).astype(BF16)

    pl.semaphore_wait(barrier, 70)

    def block(ref, i):
        return ref.at[pl.ds(pl.multiple_of(i * 16, 16), 16)]

    def send_boundary(src, dst, k):
        def one(r):
            peer = dom_peer(r)
            remote(block(src, peer), block(dst, dom), a2a_send.at[k], a2a_recv.at[k],
                   {"dom": peer}).start()
        loop(1, 64, one)

    def wait_boundary(src, dst, k):
        wait(dst.at[pl.ds(0, 63 * 16)], a2a_recv.at[k])

    send_boundary(out_ref, halo_ref, 0)
    halo_ref[pl.ds(pl.multiple_of(dom * 16, 16), 16), :] = out_ref[
        pl.ds(pl.multiple_of(dom * 16, 16), 16), :]

    nb = nb_ref[...]
    entry = nb - 128
    place_of = lax.shift_left(lax.shift_right_arithmetic(entry, 3), 4) + jnp.bitwise_and(entry, 7)
    column_ids = iota((128, 1024), 1)
    count = jnp.zeros((128, 1024), F32)
    for k in range(8, 16):
        count = count + jnp.where(column_ids == place_of[:, k:k + 1], 1.0, 0.0)
    upper = pltpu.roll(count, 8, 1)
    adj_ref[0:128, :] = count.astype(BF16)
    adj_ref[128:256, :] = upper.astype(BF16)
    adjt_ref[:, 0:128] = count.T.astype(BF16)
    adjt_ref[:, 128:256] = upper.T.astype(BF16)
    own_ids = iota((128, 128), 1)
    own = jnp.zeros((128, 128), F32)
    for k in range(8):
        own = own + jnp.where(own_ids == nb[:, k:k + 1], 1.0, 0.0)
    own_adj = own.astype(BF16)
    own_adj_t = own.T.astype(BF16)
    own_sum = dot(own_adj, feat)
    pre_self = dot(feat, ws_ref[...])
    lt_ref[0] = feat.astype(F32).T.astype(BF16)

    wait_boundary(out_ref, halo_ref, 0)
    halo_sum = dot(adj_ref[...], halo_ref[...])
    summed = own_sum + jnp.concatenate([halo_sum[0:128], halo_sum[128:256]], axis=1)
    agg = (summed * (1.0 / 16.0)).astype(BF16)
    pre = pre_self + dot(agg, wn_ref[...])
    grad_pre = (cot_ref[...].astype(F32) * gelu_slope(pre)).astype(BF16)

    agg_t = agg.astype(F32).T
    agg_t = jnp.swapaxes(agg_t.reshape(8, 8, 8, 128), 0, 1).reshape(512, 128)
    lt_ref[1] = agg_t.astype(BF16)
    scale = 65536.0 ** -0.5
    pair_out[...] = (dot(lt_ref[other], grad_pre) * scale).astype(BF16)

    def chunk(ref, i):
        return ref.at[pl.ds(pl.multiple_of(i * 64, 64), 64)]

    def send_pair(r):
        i = grp_peer(r)
        remote(chunk(pair_out, i), chunk(pair_in, i), pair_send.at[i], pair_recv.at[i],
               {"dom": sibling}).start()
    loop(1, 9, send_pair)
    own_ref[...] = dot(lt_ref[core], grad_pre) * scale

    grad_agg = (dot(grad_pre, wn_ref[...], 1, 1) * (1.0 / 16.0)).astype(BF16)
    grad_agg2 = jnp.concatenate([grad_agg[:, :256], grad_agg[:, 256:]], axis=0)
    back_ref[...] = dot(adjt_ref[...], grad_agg2).astype(BF16)

    def send_z(r):
        i = grp_peer(r)
        wait(chunk(pair_in, i), pair_recv.at[i])
        at = pl.ds(pl.multiple_of(i * 64, 64), 64)
        z_out[at, :] = (own_ref[at, :] + pair_in[at, :].astype(F32)).astype(BF16)
        remote(chunk(z_out, i), chunk(z_in, grp), z_send, z_recv, {"grp": i}).start()
    loop(1, 8, send_z)

    send_boundary(back_ref, ret_ref, 1)
    ret_ref[pl.ds(pl.multiple_of(dom * 16, 16), 16), :] = back_ref[
        pl.ds(pl.multiple_of(dom * 16, 16), 16), :]
    base_ref[...] = dot(grad_pre, ws_ref[...], 1, 1) + dot(own_adj_t, grad_agg)

    wait(chunk(pair_in, grp), pair_recv.at[grp])
    mine = pl.ds(pl.multiple_of(grp * 64, 64), 64)
    total = own_ref[mine, :] + pair_in[mine, :].astype(F32)
    wait(z_in.at[pl.ds(0, 7 * 64)], z_recv)
    for r in range(1, 8):
        total = total + z_in[pl.ds(pl.multiple_of(grp_peer(r) * 64, 64), 64), :].astype(F32)

    for q in range(32):
        a, b = q // 4, q % 4
        xy_out[q] = total[8 * a:8 * a + 8, 128 * b:128 * b + 128]

    def send_xy(r):
        q = place_peer(r)
        remote(xy_out.at[q], xy_in.at[place], xy_send, xy_recv, {"dom": 2 * q + core}).start()
    loop(1, 32, send_xy)

    wait_boundary(back_ref, ret_ref, 1)
    returned = dot(sel_ref[...], ret_ref[...])
    gfeat_ref[...] = (
        base_ref[...] + jnp.concatenate([returned[0:128], returned[128:256]], axis=1)
    ).astype(BF16)

    wait(xy_in.at[pl.ds(0, 31)], xy_recv)
    xy_in[place] = xy_out[place]
    done = jnp.sum(xy_in[...], axis=0)

    @pl.when(core == 0)
    def _():
        ag_ref[place] = done

        def send_one(r):
            q = place_peer(r)
            remote(ag_ref.at[place], ag_ref.at[place], ag1_send, ag1_recv, {"dom": 2 * q}).start()
        loop(1, 32, send_one)
        wait(ag_ref.at[pl.ds(0, 31)], ag1_recv)
        wait(ag_ref.at[pl.ds(0, 31)], ag1_send)
        rows = [jnp.concatenate([ag_ref[4 * a + b] for b in range(4)], axis=1) for a in range(8)]
        full_ref[0, mine, :] = jnp.concatenate(rows, axis=0).astype(BF16)

        def send_two(r):
            remote(full_ref.at[0, mine], full_ref.at[0, mine], ag2_send, ag2_recv,
                   {"grp": grp_peer(r)}).start()
        loop(1, 8, send_two)
        wait(full_ref.at[0, pl.ds(0, 7 * 64)], ag2_recv)
        wait(full_ref.at[0, pl.ds(0, 7 * 64)], ag2_send)

    @pl.when(core == 1)
    def _():
        agz_ref[grp] = done

        def send_one(r):
            remote(agz_ref.at[grp], agz_ref.at[grp], ag1_send, ag1_recv,
                   {"grp": grp_peer(r)}).start()
        loop(1, 8, send_one)
        wait(agz_ref.at[pl.ds(0, 7)], ag1_recv)
        wait(agz_ref.at[pl.ds(0, 7)], ag1_send)
        a = place // 4
        b = lax.rem(place, 4)
        at = (pl.ds(pl.multiple_of(a * 64, 64), 64), pl.ds(pl.multiple_of(b * 128, 128), 128))
        full_ref[1, at[0], at[1]] = agz_ref[...].reshape(64, 128).astype(BF16)

        def send_two(r):
            q = place_peer(r)
            remote(full_ref.at[1, at[0], at[1]], full_ref.at[1, at[0], at[1]], ag2_send, ag2_recv,
                   {"dom": 2 * q + 1}).start()
        loop(1, 32, send_two)
        wait(full_ref.at[1, pl.ds(0, 496)], ag2_recv)
        wait(full_ref.at[1, pl.ds(0, 496)], ag2_send)

    last = remote(full_ref.at[core], full_ref.at[core], fin_send, fin_recv, {"dom": sibling})
    last.start()

    wait(out_ref.at[pl.ds(0, 63 * 16)], a2a_send.at[0])
    wait(back_ref.at[pl.ds(0, 63 * 16)], a2a_send.at[1])
    loop(0, 8, lambda i: wait(chunk(pair_out, i), pair_send.at[i]))
    wait(z_out.at[pl.ds(0, 7 * 64)], z_send)
    wait(xy_out.at[pl.ds(0, 31)], xy_send)
    last.wait()
    gw_ref[...] = full_ref[...]


def local(features, w_self, w_neigh, cotangent, neighbors, send_rows, send_count):
    vmem = pl.BlockSpec(memory_space=pltpu.VMEM)
    dma = pltpu.SemaphoreType.DMA
    grad_features, grads = pl.pallas_call(
        kernel,
        out_shape=(
            jax.ShapeDtypeStruct((128, 512), BF16),
            jax.ShapeDtypeStruct((2, 512, 512), BF16),
        ),
        in_specs=[vmem] * 7,
        out_specs=(vmem, vmem),
        scratch_shapes=[
            pltpu.VMEM((256, 1024), BF16),
            pltpu.VMEM((256, 1024), BF16),
            pltpu.VMEM((1024, 256), BF16),
            pltpu.VMEM((1024, 256), BF16),
            pltpu.VMEM((1024, 256), BF16),
            pltpu.VMEM((1024, 256), BF16),
            pltpu.VMEM((1024, 256), BF16),
            pltpu.VMEM((2, 512, 128), BF16),
            pltpu.VMEM((512, 512), F32),
            pltpu.VMEM((512, 512), BF16),
            pltpu.VMEM((512, 512), BF16),
            pltpu.VMEM((512, 512), BF16),
            pltpu.VMEM((512, 512), BF16),
            pltpu.VMEM((32, 8, 128), F32),
            pltpu.VMEM((32, 8, 128), F32),
            pltpu.VMEM((32, 8, 128), F32),
            pltpu.VMEM((8, 8, 128), F32),
            pltpu.VMEM((2, 512, 512), BF16),
            pltpu.VMEM((128, 512), F32),
            dma((2,)), dma((2,)), dma((8,)), dma((8,)), dma, dma, dma, dma,
            dma, dma, dma, dma, dma, dma,
        ],
        compiler_params=pltpu.CompilerParams(
            collective_id=0, has_side_effects=True, vmem_limit_bytes=40 << 20
        ),
        name="sage_backward",
    )(
        features, w_self, w_neigh, cotangent, neighbors,
        send_rows.reshape(64, 8), send_count.reshape(1, 64),
    )
    return grad_features, grads[0].astype(F32), grads[1].astype(F32)


def solution(mesh):
    placed = (
        P(("grp", "dom"), None),
        P(),
        P(),
        P(("grp", "dom"), None),
        P(("grp", "dom"), None),
        P("grp", "dom", None, None),
        P("grp", "dom", None),
    )
    return jax.shard_map(
        local,
        mesh=mesh,
        in_specs=placed,
        out_specs=(P(("grp", "dom"), None), P(), P()),
        check_vma=False,
    )
```

```python
import functools

import jax
import jax.numpy as jnp
from jax import lax
from jax.experimental import pallas as pl
from jax.experimental.pallas import tpu as pltpu
from jax.sharding import PartitionSpec as P

MESH = pl.DeviceIdType.MESH
F32 = jnp.float32
BF16 = jnp.bfloat16


def dot(left, right, left_dim=1, right_dim=0):
    return lax.dot_general(
        left, right, (((left_dim,), (right_dim,)), ((), ())), preferred_element_type=F32
    )


def iota(shape, dim):
    return lax.broadcasted_iota(jnp.int32, shape, dim)


def gelu_slope(v):
    root = 0.7978845608028654
    square = v * v
    t = jnp.tanh(root * (v + 0.044715 * square * v))
    return 0.5 * (1.0 + t) + (0.5 * root) * v * (1.0 - t * t) * (1.0 + 0.134145 * square)


def kernel(
    feat_hbm, ws_hbm, wn_hbm, cot_hbm, nb_hbm, rows_hbm, count_hbm,
    gfeat_ref, gw_ref,
    feat_ref, ws_ref, wn_ref, cot_ref, nb_ref, rows_ref, count_ref,
    sel_ref, adj_ref, adjt_ref, out_ref, halo_ref, back_ref, ret_ref,
    lt_ref, own_ref, pair_out, pair_in, one_out, one_in, two_out, two_in, y_ref, base_ref,
    load_sem, a2a_send, a2a_recv, pair_send, pair_recv, one_send, one_recv, two_send, two_recv,
    y_send, y_recv, ag1_send, ag1_recv, ag2_send, ag2_recv, fin_send, fin_recv,
):
    grp = lax.axis_index("grp")
    dom = lax.axis_index("dom")
    core = lax.rem(dom, 2)
    y = lax.rem(dom // 2, 8)
    x = dom // 16
    other = 1 - core
    sibling = {"dom": dom + 1 - 2 * core}

    def at_x(i):
        return {"dom": i * 16 + y * 2 + core}

    def at_y(i):
        return {"dom": x * 16 + i * 2 + core}

    def at_z(i):
        return {"grp": i}

    def dom_peer(r):
        return lax.rem(dom + r, 64)

    def loop(first, last, body):
        lax.fori_loop(first, last, lambda i, c: (body(i), c)[1], 0)

    def remote(src, dst, send, recv, device):
        return pltpu.make_async_remote_copy(
            src_ref=src, dst_ref=dst, send_sem=send, recv_sem=recv,
            device_id=device, device_id_type=MESH,
        )

    def wait(ref, sem):
        pltpu.make_async_copy(ref, ref, sem).wait()

    def part(i, size):
        return pl.ds(pl.multiple_of(i * size, size), size)

    loads = [
        pltpu.make_async_copy(src, dst, load_sem.at[i])
        for i, (src, dst) in enumerate([
            (rows_hbm, rows_ref), (count_hbm, count_ref), (feat_hbm, feat_ref), (nb_hbm, nb_ref),
            (ws_hbm, ws_ref), (wn_hbm, wn_ref), (cot_hbm, cot_ref),
        ])
    ]
    for load in loads:
        load.start()

    barrier = pltpu.get_barrier_semaphore()
    loop(1, 64, lambda r: pl.semaphore_signal(
        barrier, inc=1, device_id={"dom": dom_peer(r)}, device_id_type=MESH))
    loop(1, 8, lambda r: pl.semaphore_signal(
        barrier, inc=1, device_id=at_z(lax.rem(grp + r, 8)), device_id_type=MESH))

    col = iota((1, 1024), 1)
    slot_of = jnp.bitwise_and(col, 7)
    half_of = jnp.bitwise_and(lax.shift_right_logical(col, 3), 1)
    in_peer = (iota((64, 1024), 0) == lax.shift_right_logical(col, 4)).astype(BF16)
    for load in loads[:3]:
        load.wait()
    counts = jnp.broadcast_to(count_ref[...], (8, 64))
    table = jnp.concatenate([rows_ref[...], counts], axis=0).astype(F32).astype(BF16)
    spread = dot(table, in_peer)
    row = jnp.sum(jnp.where(iota((8, 1024), 0) == slot_of, spread[0:8], 0.0), axis=0, keepdims=True)
    live = spread[8:9] > slot_of.astype(F32)
    target = jnp.where(live, row + 128.0 * half_of.astype(F32), 512.0)
    sel_ref[...] = (iota((256, 1024), 0).astype(F32) == target).astype(BF16)
    feat = feat_ref[...]
    feat2 = jnp.concatenate([feat[:, :256], feat[:, 256:]], axis=0)
    out_ref[...] = dot(sel_ref[...], feat2, 0, 0).astype(BF16)

    pl.semaphore_wait(barrier, 70)

    def send_boundary(src, dst, k):
        def one(r):
            peer = dom_peer(r)
            remote(src.at[part(peer, 16)], dst.at[part(dom, 16)], a2a_send.at[k], a2a_recv.at[k],
                   {"dom": peer}).start()
        loop(1, 64, one)
        dst[part(dom, 16), :] = src[part(dom, 16), :]

    def wait_boundary(dst, k):
        wait(dst.at[pl.ds(0, 63 * 16)], a2a_recv.at[k])

    send_boundary(out_ref, halo_ref, 0)

    loads[3].wait()
    nb = nb_ref[...]
    entry = nb - 128
    place_of = lax.shift_left(lax.shift_right_arithmetic(entry, 3), 4) + jnp.bitwise_and(entry, 7)
    row_ids = iota((1024, 128), 0)
    count = jnp.zeros((1024, 128), F32)
    for k in range(8, 16):
        count = count + jnp.where(row_ids == place_of[k:k + 1, :], 1.0, 0.0)
    lower = count.T
    adjt_ref[:, 0:128] = count.astype(BF16)
    adjt_ref[:, 128:256] = pltpu.roll(count, 8, 0).astype(BF16)
    adj_ref[0:128, :] = lower.astype(BF16)
    adj_ref[128:256, :] = pltpu.roll(lower, 8, 1).astype(BF16)
    own_ids = iota((128, 128), 0)
    own_t = jnp.zeros((128, 128), F32)
    for k in range(8):
        own_t = own_t + jnp.where(own_ids == nb[k:k + 1, :], 1.0, 0.0)
    own_adj = own_t.T.astype(BF16)
    own_adj_t = own_t.astype(BF16)
    own_sum = dot(own_adj, feat)
    lt_ref[0] = feat.astype(F32).T.astype(BF16)
    for load in loads[4:]:
        load.wait()
    pre_self = dot(feat, ws_ref[...])

    wait_boundary(halo_ref, 0)
    halo_sum = dot(adj_ref[...], halo_ref[...])
    summed = own_sum + jnp.concatenate([halo_sum[0:128], halo_sum[128:256]], axis=1)
    agg = (summed * (1.0 / 16.0)).astype(BF16)
    pre = pre_self + dot(agg, wn_ref[...])
    grad_pre = (cot_ref[...].astype(F32) * gelu_slope(pre)).astype(BF16)

    lt_ref[1] = agg.astype(F32).T.astype(BF16)
    scale = 65536.0 ** -0.5
    pair_out[...] = (dot(lt_ref[other], grad_pre) * scale).astype(BF16)

    def send_pair(first):
        def one(r):
            i = lax.rem(first + r, 8)
            remote(pair_out.at[part(i, 64)], pair_in.at[part(i, 64)], pair_send.at[i],
                   pair_recv.at[i], sibling).start()
        loop(0, 8, one)

    send_pair(lax.rem(core * (grp + 1) + other * (x * 2 + 2), 8))
    own_ref[...] = dot(lt_ref[core], grad_pre) * scale

    grad_agg = (dot(grad_pre, wn_ref[...], 1, 1) * (1.0 / 16.0)).astype(BF16)
    grad_agg2 = jnp.concatenate([grad_agg[:, :256], grad_agg[:, 256:]], axis=0)
    back_ref[...] = dot(adjt_ref[...], grad_agg2).astype(BF16)

    def features_gradient():
        wait_boundary(ret_ref, 1)
        returned = dot(sel_ref[...], ret_ref[...])
        gfeat_ref[...] = (
            base_ref[...] + jnp.concatenate([returned[0:128], returned[128:256]], axis=1)
        ).astype(BF16)

    def sum_matrix(c, n1, me1, at1, n2, me2, at2):
        rows1 = 512 // n1
        rows2 = rows1 // n2

        def send_first(r):
            i = lax.rem(me1 + r, n1)
            for j in range(rows1 // 64):
                piece = i * (rows1 // 64) + j
                wait(pair_in.at[part(piece, 64)], pair_recv.at[piece])
            rows = part(i, rows1)
            one_out[rows, :] = (own_ref[rows, :] + pair_in[rows, :].astype(F32)).astype(BF16)
            remote(one_out.at[rows], one_in.at[part(me1, rows1)], one_send, one_recv, at1(i)).start()
        loop(1, n1, send_first)

        send_boundary(back_ref, ret_ref, 1)
        base_ref[...] = dot(grad_pre, ws_ref[...], 1, 1) + dot(own_adj_t, grad_agg)

        for j in range(rows1 // 64):
            piece = me1 * (rows1 // 64) + j
            wait(pair_in.at[part(piece, 64)], pair_recv.at[piece])
        mine = part(me1, rows1)
        total = own_ref[mine, :] + pair_in[mine, :].astype(F32)
        wait(one_in.at[pl.ds(0, 512 - rows1)], one_recv)
        for r in range(1, n1):
            total = total + one_in[part(lax.rem(me1 + r, n1), rows1), :].astype(F32)

        own_ref[0:rows1, :] = total
        two_out[0:rows1, :] = total.astype(BF16)

        def send_second(r):
            i = lax.rem(me2 + r, n2)
            remote(two_out.at[part(i, rows2)], two_in.at[part(me2, rows2)], two_send, two_recv,
                   at2(i)).start()
        loop(1, n2, send_second)
        wait(two_in.at[pl.ds(0, rows1 - rows2)], two_recv)
        small = own_ref[part(me2, rows2), :]
        for r in range(1, n2):
            small = small + two_in[part(lax.rem(me2 + r, n2), rows2), :].astype(F32)

        y_ref[part(y, 16), :] = small.astype(BF16)

        def send_y(r):
            remote(y_ref.at[part(y, 16)], y_ref.at[part(y, 16)], y_send, y_recv,
                   at_y(lax.rem(y + r, 8))).start()
        loop(1, 8, send_y)
        wait(y_ref.at[pl.ds(0, 7 * 16)], y_recv)
        done = y_ref[0:16, :].astype(F32)
        for i in range(1, 8):
            done = done + y_ref[16 * i:16 * i + 16, :].astype(F32)
        at_two = pl.ds(pl.multiple_of(me1 * rows1 + me2 * rows2, rows2), rows2)
        gw_ref[c, at_two, :] = done.astype(BF16)

        def gather_two(r):
            remote(gw_ref.at[c, at_two], gw_ref.at[c, at_two], ag1_send, ag1_recv,
                   at2(lax.rem(me2 + r, n2))).start()
        loop(1, n2, gather_two)
        features_gradient()
        wait(gw_ref.at[c, pl.ds(0, rows1 - rows2)], ag1_recv)

        def gather_one(r):
            remote(gw_ref.at[c, mine], gw_ref.at[c, mine], ag2_send, ag2_recv.at[me1],
                   at1(lax.rem(me1 + r, n1))).start()
        loop(1, n1, gather_one)

        def forward(i):
            for j in range(rows1 // 64):
                piece = i * (rows1 // 64) + j
                rows = part(piece, 64)
                remote(gw_ref.at[c, rows], gw_ref.at[c, rows], fin_send.at[piece],
                       fin_recv.at[piece], sibling).start()
        forward(me1)

        def arrived(r):
            i = lax.rem(me1 + r, n1)
            wait(gw_ref.at[c, part(i, rows1)], ag2_recv.at[i])
            forward(i)
        loop(1, n1, arrived)

        wait(one_out.at[pl.ds(0, 512 - rows1)], one_send)
        wait(two_out.at[pl.ds(0, rows1 - rows2)], two_send)
        wait(gw_ref.at[c, pl.ds(0, rows1 - rows2)], ag1_send)
        wait(gw_ref.at[c, pl.ds(0, 512 - rows1)], ag2_send)

    @pl.when(core == 0)
    def _():
        sum_matrix(0, 8, grp, at_z, 4, x, at_x)

    @pl.when(core == 1)
    def _():
        sum_matrix(1, 4, x, at_x, 8, grp, at_z)

    wait(out_ref.at[pl.ds(0, 63 * 16)], a2a_send.at[0])
    wait(back_ref.at[pl.ds(0, 63 * 16)], a2a_send.at[1])
    wait(y_ref.at[pl.ds(0, 7 * 16)], y_send)

    def finish(i):
        wait(pair_out.at[part(i, 64)], pair_send.at[i])
        wait(gw_ref.at[core, part(i, 64)], fin_send.at[i])
        wait(gw_ref.at[other, part(i, 64)], fin_recv.at[i])
    loop(0, 8, finish)


def write_kernel(gfeat_in, gw_in, gfeat_ref, gws_ref, gwn_ref, wide_ref, sem):
    copies = [pltpu.make_async_copy(gfeat_in, gfeat_ref, sem.at[0])]
    copies[0].start()
    for c, ref in enumerate((gws_ref, gwn_ref)):
        for half in range(2):
            rows = pl.ds(256 * half, 256)
            wide_ref[c, rows, :] = gw_in[c, rows, :].astype(F32)
            copy = pltpu.make_async_copy(
                wide_ref.at[c, rows], ref.at[rows], sem.at[1 + 2 * c + half])
            copy.start()
            copies.append(copy)
    for copy in copies:
        copy.wait()


def local(features, w_self, w_neigh, cotangent, neighbors, send_rows, send_count):
    vmem = pl.BlockSpec(memory_space=pltpu.VMEM)
    hbm = pl.BlockSpec(memory_space=pltpu.HBM)
    dma = pltpu.SemaphoreType.DMA
    grad_features, grads = pl.pallas_call(
        kernel,
        out_shape=(
            pltpu.VMEM((128, 512), BF16),
            pltpu.VMEM((2, 512, 512), BF16),
        ),
        in_specs=[hbm] * 7,
        out_specs=(vmem, vmem),
        scratch_shapes=[
            pltpu.VMEM((128, 512), BF16),
            pltpu.VMEM((512, 512), BF16),
            pltpu.VMEM((512, 512), BF16),
            pltpu.VMEM((128, 512), BF16),
            pltpu.VMEM((16, 128), jnp.int32),
            pltpu.VMEM((8, 64), jnp.int32),
            pltpu.VMEM((1, 64), jnp.int32),
            pltpu.VMEM((256, 1024), BF16),
            pltpu.VMEM((256, 1024), BF16),
            pltpu.VMEM((1024, 256), BF16),
            pltpu.VMEM((1024, 256), BF16),
            pltpu.VMEM((1024, 256), BF16),
            pltpu.VMEM((1024, 256), BF16),
            pltpu.VMEM((1024, 256), BF16),
            pltpu.VMEM((2, 512, 128), BF16),
            pltpu.VMEM((512, 512), F32),
            pltpu.VMEM((512, 512), BF16),
            pltpu.VMEM((512, 512), BF16),
            pltpu.VMEM((512, 512), BF16),
            pltpu.VMEM((512, 512), BF16),
            pltpu.VMEM((128, 512), BF16),
            pltpu.VMEM((128, 512), BF16),
            pltpu.VMEM((128, 512), BF16),
            pltpu.VMEM((128, 512), F32),
            dma((7,)), dma((2,)), dma((2,)), dma((8,)), dma((8,)), dma, dma, dma, dma,
            dma, dma, dma, dma, dma, dma((8,)), dma((8,)), dma((8,)),
        ],
        compiler_params=pltpu.CompilerParams(
            collective_id=0, has_side_effects=True, vmem_limit_bytes=40 << 20
        ),
        name="sage_backward",
    )(*(
        pltpu.with_memory_space_constraint(array, pltpu.HBM)
        for array in (
            features, w_self, w_neigh, cotangent, neighbors.T,
            send_rows.reshape(64, 8).T, send_count.reshape(1, 64),
        )
    ))
    return pl.pallas_call(
        write_kernel,
        out_shape=(
            jax.ShapeDtypeStruct((128, 512), BF16),
            jax.ShapeDtypeStruct((512, 512), F32),
            jax.ShapeDtypeStruct((512, 512), F32),
        ),
        in_specs=[vmem, vmem],
        out_specs=(hbm, hbm, hbm),
        scratch_shapes=[pltpu.VMEM((2, 512, 512), F32), dma((5,))],
        compiler_params=pltpu.CompilerParams(vmem_limit_bytes=8 << 20),
        name="write_results",
    )(grad_features, grads)


def solution(mesh):
    placed = (
        P(("grp", "dom"), None),
        P(),
        P(),
        P(("grp", "dom"), None),
        P(("grp", "dom"), None),
        P("grp", "dom", None, None),
        P("grp", "dom", None),
    )
    return jax.shard_map(
        local,
        mesh=mesh,
        in_specs=placed,
        out_specs=(P(("grp", "dom"), None), P(), P()),
        check_vma=False,
    )
```

```python
import functools

import jax
import jax.numpy as jnp
from jax import lax
from jax.experimental import pallas as pl
from jax.experimental.pallas import tpu as pltpu
from jax.sharding import PartitionSpec as P

MESH = pl.DeviceIdType.MESH
F32 = jnp.float32
BF16 = jnp.bfloat16


STRIPS = ((0, 256, "xzy"), (256, 128, "zxy"), (384, 128, "yxz"))
BATCHES = (((1, 16, 1),), ((16, 32, 1),), ((32, 48, 1),), ((48, 64, 1),))


def dot(left, right, left_dim=1, right_dim=0):
    return lax.dot_general(
        left, right, (((left_dim,), (right_dim,)), ((), ())), preferred_element_type=F32
    )


def iota(shape, dim):
    return lax.broadcasted_iota(jnp.int32, shape, dim)


def gelu_slope(v):
    root = 0.7978845608028654
    square = v * v
    t = jnp.tanh(root * (v + 0.044715 * square * v))
    return 0.5 * (1.0 + t) + (0.5 * root) * v * (1.0 - t * t) * (1.0 + 0.134145 * square)


def kernel(
    feat_hbm, ws_hbm, wn_hbm, cot_hbm, nb_hbm, rows_hbm, count_hbm,
    gfeat_ref, gw_ref,
    feat_ref, ws_ref, wn_ref, cot_ref, nb_ref, rows_ref, count_ref,
    sel_ref, adj_ref, adjt_ref, out_ref, halo_ref, back_ref, ret_ref,
    lt_ref, own_ref, pair_out, pair_in, one_out, one_in, sum_ref, two_out, two_in, three_ref, base_ref,
    load_sem, a2a_send, a2a_recv, pair_send, pair_recv, one_send, one_recv, two_send, two_recv,
    three_send, three_recv, ag1_send, ag1_recv, ag2_send, ag2_recv, fin_send, fin_recv,
):
    grp = lax.axis_index("grp")
    dom = lax.axis_index("dom")
    core = lax.rem(dom, 2)
    other = 1 - core
    sibling = {"dom": dom + 1 - 2 * core}
    y = lax.rem(dom // 2, 8)
    x = dom // 16

    axis_x = (4, x, lambda i: {"dom": i * 16 + y * 2 + core})
    axis_y = (8, y, lambda i: {"dom": x * 16 + i * 2 + core})
    axis_z = (8, grp, lambda i: {"grp": i})
    axes = {"x": axis_x, "y": axis_y, "z": axis_z}
    strips = tuple(
        (first, width) + tuple(axes[name] for name in order) for first, width, order in STRIPS
    )

    def dom_peer(r):
        return lax.rem(dom + r, 64)

    def loop(first, last, body):
        lax.fori_loop(first, last, lambda i, c: (body(i), c)[1], 0)

    def remote(src, dst, send, recv, device):
        return pltpu.make_async_remote_copy(
            src_ref=src, dst_ref=dst, send_sem=send, recv_sem=recv,
            device_id=device, device_id_type=MESH,
        )

    def wait(ref, sem):
        pltpu.make_async_copy(ref, ref, sem).wait()

    def part(i, size):
        return pl.ds(pl.multiple_of(i * size, size), size)

    loads = [
        pltpu.make_async_copy(src, dst, load_sem.at[i])
        for i, (src, dst) in enumerate([
            (rows_hbm, rows_ref), (count_hbm, count_ref), (feat_hbm, feat_ref), (nb_hbm, nb_ref),
            (ws_hbm, ws_ref), (wn_hbm, wn_ref), (cot_hbm, cot_ref),
        ])
    ]
    for load in loads:
        load.start()

    barrier = pltpu.get_barrier_semaphore()
    with jax.named_scope("greet"):
        loop(1, 64, lambda r: pl.semaphore_signal(
            barrier, inc=1, device_id={"dom": dom_peer(r)}, device_id_type=MESH))
        loop(1, 8, lambda r: pl.semaphore_signal(
            barrier, inc=1, device_id={"grp": lax.rem(grp + r, 8)}, device_id_type=MESH))

    with jax.named_scope("outgoing"):
        col = iota((1, 1024), 1)
        slot_of = jnp.bitwise_and(col, 7)
        half_of = jnp.bitwise_and(lax.shift_right_logical(col, 3), 1)
        in_peer = (iota((64, 1024), 0) == lax.shift_right_logical(col, 4)).astype(BF16)
        for load in loads[:3]:
            load.wait()
        counts = jnp.broadcast_to(count_ref[...], (8, 64))
        table = jnp.concatenate([rows_ref[...], counts], axis=0).astype(F32).astype(BF16)
        spread = dot(table, in_peer)
        row = jnp.sum(
            jnp.where(iota((8, 1024), 0) == slot_of, spread[0:8], 0.0), axis=0, keepdims=True)
        live = spread[8:9] > slot_of.astype(F32)
        target = jnp.where(live, row + 128.0 * half_of.astype(F32), 512.0)
        sel_ref[...] = (iota((256, 1024), 0).astype(F32) == target).astype(BF16)
        feat = feat_ref[...]
        feat2 = jnp.concatenate([feat[:, :256], feat[:, 256:]], axis=0)
        out_ref[...] = dot(sel_ref[...], feat2, 0, 0).astype(BF16)

    with jax.named_scope("barrier"):
        pl.semaphore_wait(barrier, 70)

    def send_boundary(src, dst, k, *distances):
        def one(r):
            peer = dom_peer(r)
            remote(src.at[part(peer, 16)], dst.at[part(dom, 16)], a2a_send.at[k], a2a_recv.at[k],
                   {"dom": peer}).start()
        for first, last, step in distances:
            loop(0, (last - first) // step, lambda i: one(first + step * i))

    def keep_boundary(src, dst):
        dst[part(dom, 16), :] = src[part(dom, 16), :]

    def wait_boundary(dst, k):
        wait(dst.at[pl.ds(0, 63 * 16)], a2a_recv.at[k])

    with jax.named_scope("send_rows"):
        send_boundary(out_ref, halo_ref, 0, (1, 64, 1))
        keep_boundary(out_ref, halo_ref)

    with jax.named_scope("adjacency"):
        loads[3].wait()
        nb = nb_ref[...]
        entry = nb - 128
        place_of = (
            lax.shift_left(lax.shift_right_arithmetic(entry, 3), 4) + jnp.bitwise_and(entry, 7))
        row_ids = iota((1024, 128), 0)
        count = jnp.zeros((1024, 128), F32)
        for k in range(8, 16):
            count = count + jnp.where(row_ids == place_of[k:k + 1, :], 1.0, 0.0)
        lower = count.T
        adjt_ref[:, 0:128] = count.astype(BF16)
        adjt_ref[:, 128:256] = pltpu.roll(count, 8, 0).astype(BF16)
        adj_ref[0:128, :] = lower.astype(BF16)
        adj_ref[128:256, :] = pltpu.roll(lower, 8, 1).astype(BF16)
        own_ids = iota((128, 128), 0)
        own_t = jnp.zeros((128, 128), F32)
        for k in range(8):
            own_t = own_t + jnp.where(own_ids == nb[k:k + 1, :], 1.0, 0.0)
        own_adj = own_t.T.astype(BF16)
        own_adj_t = own_t.astype(BF16)
        own_sum = dot(own_adj, feat)
        lt_ref[0] = feat.astype(F32).T.astype(BF16)
        for load in loads[4:]:
            load.wait()
        pre_self = dot(feat, ws_ref[...])

    with jax.named_scope("wait_rows"):
        wait_boundary(halo_ref, 0)
    with jax.named_scope("grad_pre"):
        halo_sum = dot(adj_ref[...], halo_ref[...])
        summed = own_sum + jnp.concatenate([halo_sum[0:128], halo_sum[128:256]], axis=1)
        agg = (summed * (1.0 / 16.0)).astype(BF16)
        pre = pre_self + dot(agg, wn_ref[...])
        grad_pre = (cot_ref[...].astype(F32) * gelu_slope(pre)).astype(BF16)

    with jax.named_scope("weight_grads"):
        lt_ref[1] = agg.astype(F32).T.astype(BF16)
        scale = 65536.0 ** -0.5
        pair_out[...] = (dot(lt_ref[other], grad_pre) * scale).astype(BF16)
        for r in range(4):
            i = lax.rem(x + 1 + r, 4)
            remote(pair_out.at[part(i, 128)], pair_in.at[part(i, 128)], pair_send.at[i],
                   pair_recv.at[i], sibling).start()
        own_ref[...] = dot(lt_ref[core], grad_pre) * scale

    with jax.named_scope("boundary_grads"):
        grad_agg = (dot(grad_pre, wn_ref[...], 1, 1) * (1.0 / 16.0)).astype(BF16)
        grad_agg2 = jnp.concatenate([grad_agg[:, :256], grad_agg[:, 256:]], axis=0)
        back_ref[...] = dot(adjt_ref[...], grad_agg2).astype(BF16)

    def send_one(s, i):
        first, width, (n, me, at), _, _ = strips[s]
        rows = part(i, 512 // n)
        cols = pl.ds(first, width)
        one_out[s][rows, :] = (
            own_ref[rows, cols] + pair_in[rows, cols].astype(F32)).astype(BF16)

        @pl.when(i != me)
        def _():
            remote(one_out[s].at[rows], one_in[s].at[part(me, 512 // n)], one_send.at[s],
                   one_recv.at[s], at(i)).start()

    with jax.named_scope("step_one"):
        for r in range(4):
            i = lax.rem(x + 1 + r, 4)
            wait(pair_in.at[part(i, 128)], pair_recv.at[i])
            for s, (_, _, (n1, _, _), _, _) in enumerate(strips):
                for j in range(n1 // 4):
                    send_one(s, n1 // 4 * i + j)

    with jax.named_scope("send_grads"):
        send_boundary(back_ref, ret_ref, 1, *BATCHES[0])
        keep_boundary(back_ref, ret_ref)
    with jax.named_scope("base"):
        base_ref[...] = dot(grad_pre, ws_ref[...], 1, 1) + dot(own_adj_t, grad_agg)

    for s, (first, width, (n1, me1, _), (n2, me2, at2), _) in enumerate(strips):
        with jax.named_scope("step_two_%d" % s):
            rows1 = 512 // n1
            mine = part(me1, rows1)
            cols = pl.ds(first, width)
            total = own_ref[mine, cols] + pair_in[mine, cols].astype(F32)
            wait(one_in[s].at[pl.ds(0, 512 - rows1)], one_recv.at[s])
            for r in range(1, n1):
                total = total + one_in[s][part(lax.rem(me1 + r, n1), rows1), :].astype(F32)
            sum_ref[s][...] = total
            two_out[s][...] = total.astype(BF16)
            for r in range(1, n2):
                i = lax.rem(me2 + r, n2)
                remote(two_out[s].at[part(i, 16)], two_in[s].at[part(me2, 16)], two_send.at[s],
                       two_recv.at[s], at2(i)).start()

    send_boundary(back_ref, ret_ref, 1, *BATCHES[1])

    for s, (_, _, _, (n2, me2, _), (n3, me3, at3)) in enumerate(strips):
        with jax.named_scope("step_three_%d" % s):
            small = sum_ref[s][part(me2, 16), :]
            wait(two_in[s].at[pl.ds(0, 16 * (n2 - 1))], two_recv.at[s])
            for r in range(1, n2):
                small = small + two_in[s][part(lax.rem(me2 + r, n2), 16), :].astype(F32)
            three_ref[s][part(me3, 16), :] = small.astype(BF16)
            for r in range(1, n3):
                here = three_ref[s].at[part(me3, 16)]
                remote(here, here, three_send.at[s], three_recv.at[s],
                       at3(lax.rem(me3 + r, n3))).start()

    send_boundary(back_ref, ret_ref, 1, *BATCHES[2])

    def final(s, rows, count):
        first, width = strips[s][:2]
        return gw_ref.at[core, pl.ds(rows, count), pl.ds(first, width)]

    for s, (first, width, (n1, me1, _), (n2, me2, at2), (n3, _, _)) in enumerate(strips):
        with jax.named_scope("gather_one_%d" % s):
            wait(three_ref[s].at[pl.ds(0, 16 * (n3 - 1))], three_recv.at[s])
            done = three_ref[s][0:16, :].astype(F32)
            for i in range(1, n3):
                done = done + three_ref[s][16 * i:16 * i + 16, :].astype(F32)
            row = pl.multiple_of(me1 * (512 // n1) + me2 * 16, 16)
            gw_ref[core, pl.ds(row, 16), pl.ds(first, width)] = done.astype(BF16)
            for r in range(1, n2):
                remote(final(s, row, 16), final(s, row, 16), ag1_send.at[s], ag1_recv.at[s],
                       at2(lax.rem(me2 + r, n2))).start()

    send_boundary(back_ref, ret_ref, 1, *BATCHES[3])

    def forward(s, unit, row, count):
        remote(final(s, row, count), final(s, row, count), fin_send.at[s, unit],
               fin_recv.at[s, unit], sibling).start()

    for s, (_, _, (n1, me1, at1), (n2, _, _), _) in enumerate(strips):
        with jax.named_scope("gather_two_%d" % s):
            rows1 = 512 // n1
            wait(final(s, 0, 16 * (n2 - 1)), ag1_recv.at[s])
            row = pl.multiple_of(me1 * rows1, rows1)
            for r in range(1, n1):
                unit = me1 if n1 == 4 else 0
                remote(final(s, row, rows1), final(s, row, rows1), ag2_send.at[s],
                       ag2_recv.at[s, unit], at1(lax.rem(me1 + r, n1))).start()
            if n1 == 4:
                forward(s, me1, row, rows1)
    with jax.named_scope("forward"):
        for s, (_, _, (n1, me1, _), _, _) in enumerate(strips):
            if n1 == 4:
                for r in range(1, 4):
                    i = lax.rem(me1 + r, 4)
                    row = pl.multiple_of(i * 128, 128)
                    wait(final(s, row, 128), ag2_recv.at[s, i])
                    forward(s, i, row, 128)
            else:
                wait(final(s, 0, 448), ag2_recv.at[s, 0])
                forward(s, 0, 0, 512)

    with jax.named_scope("wait_grads"):
        wait_boundary(ret_ref, 1)
    with jax.named_scope("feature_grads"):
        returned = dot(sel_ref[...], ret_ref[...])
        gfeat_ref[...] = (
            base_ref[...] + jnp.concatenate([returned[0:128], returned[128:256]], axis=1)
        ).astype(BF16)

    with jax.named_scope("finish"):
        wait(out_ref.at[pl.ds(0, 63 * 16)], a2a_send.at[0])
        wait(back_ref.at[pl.ds(0, 63 * 16)], a2a_send.at[1])
        for i in range(4):
            wait(pair_out.at[pl.ds(128 * i, 128)], pair_send.at[i])
        for s, (_, _, (n1, _, _), (n2, _, _), (n3, _, _)) in enumerate(strips):
            rows1 = 512 // n1
            wait(one_out[s].at[pl.ds(0, 512 - rows1)], one_send.at[s])
            wait(two_out[s].at[pl.ds(0, 16 * (n2 - 1))], two_send.at[s])
            wait(three_ref[s].at[pl.ds(0, 16 * (n3 - 1))], three_send.at[s])
            wait(final(s, 0, 16 * (n2 - 1)), ag1_send.at[s])
            wait(final(s, 0, 512 - rows1), ag2_send.at[s])
            units = 4 if n1 == 4 else 1
            for unit in range(units):
                wait(final(s, 0, 512 // units), fin_send.at[s, unit])
                wait(final(s, 0, 512 // units), fin_recv.at[s, unit])


def write_kernel(gfeat_in, gw_in, gfeat_ref, gws_ref, gwn_ref, wide_ref, sem):
    copies = [pltpu.make_async_copy(gfeat_in, gfeat_ref, sem.at[0])]
    copies[0].start()
    for c, ref in enumerate((gws_ref, gwn_ref)):
        for half in range(2):
            rows = pl.ds(256 * half, 256)
            wide_ref[c, rows, :] = gw_in[c, rows, :].astype(F32)
            copy = pltpu.make_async_copy(
                wide_ref.at[c, rows], ref.at[rows], sem.at[1 + 2 * c + half])
            copy.start()
            copies.append(copy)
    for copy in copies:
        copy.wait()


def strip_scratch(shape, dtype):
    return tuple(
        pltpu.VMEM(shape(width, 4 if order[0] == "x" else 8), dtype) for _, width, order in STRIPS
    )


def local(features, w_self, w_neigh, cotangent, neighbors, send_rows, send_count):
    vmem = pl.BlockSpec(memory_space=pltpu.VMEM)
    hbm = pl.BlockSpec(memory_space=pltpu.HBM)
    dma = pltpu.SemaphoreType.DMA
    grad_features, grads = pl.pallas_call(
        kernel,
        out_shape=(
            pltpu.VMEM((128, 512), BF16),
            pltpu.VMEM((2, 512, 512), BF16),
        ),
        in_specs=[hbm] * 7,
        out_specs=(vmem, vmem),
        scratch_shapes=[
            pltpu.VMEM((128, 512), BF16),
            pltpu.VMEM((512, 512), BF16),
            pltpu.VMEM((512, 512), BF16),
            pltpu.VMEM((128, 512), BF16),
            pltpu.VMEM((16, 128), jnp.int32),
            pltpu.VMEM((8, 64), jnp.int32),
            pltpu.VMEM((1, 64), jnp.int32),
            pltpu.VMEM((256, 1024), BF16),
            pltpu.VMEM((256, 1024), BF16),
            pltpu.VMEM((1024, 256), BF16),
            pltpu.VMEM((1024, 256), BF16),
            pltpu.VMEM((1024, 256), BF16),
            pltpu.VMEM((1024, 256), BF16),
            pltpu.VMEM((1024, 256), BF16),
            pltpu.VMEM((2, 512, 128), BF16),
            pltpu.VMEM((512, 512), F32),
            pltpu.VMEM((512, 512), BF16),
            pltpu.VMEM((512, 512), BF16),
            strip_scratch(lambda w, n: (512, w), BF16),
            strip_scratch(lambda w, n: (512, w), BF16),
            strip_scratch(lambda w, n: (512 // n, w), F32),
            strip_scratch(lambda w, n: (512 // n, w), BF16),
            strip_scratch(lambda w, n: (512 // n, w), BF16),
            strip_scratch(lambda w, n: (128, w), BF16),
            pltpu.VMEM((128, 512), F32),
            dma((7,)), dma((2,)), dma((2,)), dma((4,)), dma((4,)),
            *([dma((len(STRIPS),))] * 9), *([dma((len(STRIPS), 4))] * 3),
        ],
        compiler_params=pltpu.CompilerParams(
            collective_id=0, has_side_effects=True, vmem_limit_bytes=40 << 20
        ),
        name="sage_backward",
    )(*(
        pltpu.with_memory_space_constraint(array, pltpu.HBM)
        for array in (
            features, w_self, w_neigh, cotangent, neighbors.T,
            send_rows.reshape(64, 8).T, send_count.reshape(1, 64),
        )
    ))
    return pl.pallas_call(
        write_kernel,
        out_shape=(
            jax.ShapeDtypeStruct((128, 512), BF16),
            jax.ShapeDtypeStruct((512, 512), F32),
            jax.ShapeDtypeStruct((512, 512), F32),
        ),
        in_specs=[vmem, vmem],
        out_specs=(hbm, hbm, hbm),
        scratch_shapes=[pltpu.VMEM((2, 512, 512), F32), dma((5,))],
        compiler_params=pltpu.CompilerParams(vmem_limit_bytes=8 << 20),
        name="write_results",
    )(grad_features, grads)


def solution(mesh):
    placed = (
        P(("grp", "dom"), None),
        P(),
        P(),
        P(("grp", "dom"), None),
        P(("grp", "dom"), None),
        P("grp", "dom", None, None),
        P("grp", "dom", None),
    )
    return jax.shard_map(
        local,
        mesh=mesh,
        in_specs=placed,
        out_specs=(P(("grp", "dom"), None), P(), P()),
        check_vma=False,
    )
```

```python
import functools

import jax
import jax.numpy as jnp
from jax import lax
from jax.experimental import pallas as pl
from jax.experimental.pallas import tpu as pltpu
from jax.sharding import PartitionSpec as P

MESH = pl.DeviceIdType.MESH
F32 = jnp.float32
BF16 = jnp.bfloat16


STRIPS = ((0, 256, "xzy"), (256, 128, "zxy"), (384, 128, "yxz"))
BATCHES = ((), ((1, 32, 1),), (), (), ((32, 64, 1),), ())


def dot(left, right, left_dim=1, right_dim=0):
    return lax.dot_general(
        left, right, (((left_dim,), (right_dim,)), ((), ())), preferred_element_type=F32
    )


def iota(shape, dim):
    return lax.broadcasted_iota(jnp.int32, shape, dim)


def gelu_slope(v):
    root = 0.7978845608028654
    square = v * v
    t = jnp.tanh(root * (v + 0.044715 * square * v))
    return 0.5 * (1.0 + t) + (0.5 * root) * v * (1.0 - t * t) * (1.0 + 0.134145 * square)


def kernel(
    feat_hbm, ws_hbm, wn_hbm, cot_hbm, nb_hbm, rows_hbm, count_hbm,
    gfeat_ref, gw_ref,
    feat_ref, ws_ref, wn_ref, cot_ref, nb_ref, rows_ref, count_ref,
    sel_ref, adj_ref, adjt_ref, out_ref, halo_ref, back_ref, ret_ref,
    lt_ref, own_ref, pair_out, pair_in, one_out, one_in, sum_ref, two_out, two_in, three_ref, base_ref,
    load_sem, a2a_send, a2a_recv, pair_send, pair_recv, one_send, one_recv, two_send, two_recv,
    three_send, three_recv, ag1_send, ag1_recv, ag2_send, ag2_recv, fin_send, fin_recv,
):
    grp = lax.axis_index("grp")
    dom = lax.axis_index("dom")
    core = lax.rem(dom, 2)
    other = 1 - core
    sibling = {"dom": dom + 1 - 2 * core}
    y = lax.rem(dom // 2, 8)
    x = dom // 16

    axis_x = (4, x, lambda i: {"dom": i * 16 + y * 2 + core})
    axis_y = (8, y, lambda i: {"dom": x * 16 + i * 2 + core})
    axis_z = (8, grp, lambda i: {"grp": i})
    axes = {"x": axis_x, "y": axis_y, "z": axis_z}
    strips = tuple(
        (first, width) + tuple(axes[name] for name in order) for first, width, order in STRIPS
    )

    def dom_peer(r):
        return lax.rem(dom + r, 64)

    def loop(first, last, body):
        lax.fori_loop(first, last, lambda i, c: (body(i), c)[1], 0)

    def remote(src, dst, send, recv, device):
        return pltpu.make_async_remote_copy(
            src_ref=src, dst_ref=dst, send_sem=send, recv_sem=recv,
            device_id=device, device_id_type=MESH,
        )

    def wait(ref, sem):
        pltpu.make_async_copy(ref, ref, sem).wait()

    def part(i, size):
        return pl.ds(pl.multiple_of(i * size, size), size)

    loads = [
        pltpu.make_async_copy(src, dst, load_sem.at[i])
        for i, (src, dst) in enumerate([
            (rows_hbm, rows_ref), (count_hbm, count_ref), (feat_hbm, feat_ref), (nb_hbm, nb_ref),
            (ws_hbm, ws_ref), (wn_hbm, wn_ref), (cot_hbm, cot_ref),
        ])
    ]
    for load in loads:
        load.start()

    barrier = pltpu.get_barrier_semaphore()
    with jax.named_scope("greet"):
        loop(1, 64, lambda r: pl.semaphore_signal(
            barrier, inc=1, device_id={"dom": dom_peer(r)}, device_id_type=MESH))
        loop(1, 8, lambda r: pl.semaphore_signal(
            barrier, inc=1, device_id={"grp": lax.rem(grp + r, 8)}, device_id_type=MESH))

    with jax.named_scope("outgoing"):
        col = iota((1, 1024), 1)
        slot_of = jnp.bitwise_and(col, 7)
        half_of = jnp.bitwise_and(lax.shift_right_logical(col, 3), 1)
        in_peer = (iota((64, 1024), 0) == lax.shift_right_logical(col, 4)).astype(BF16)
        for load in loads[:3]:
            load.wait()
        counts = jnp.broadcast_to(count_ref[...], (8, 64))
        table = jnp.concatenate([rows_ref[...], counts], axis=0).astype(F32).astype(BF16)
        spread = dot(table, in_peer)
        row = jnp.sum(
            jnp.where(iota((8, 1024), 0) == slot_of, spread[0:8], 0.0), axis=0, keepdims=True)
        live = spread[8:9] > slot_of.astype(F32)
        target = jnp.where(live, row + 128.0 * half_of.astype(F32), 512.0)
        sel_ref[...] = (iota((256, 1024), 0).astype(F32) == target).astype(BF16)
        feat = feat_ref[...]
        feat2 = jnp.concatenate([feat[:, :256], feat[:, 256:]], axis=0)
        out_ref[...] = dot(sel_ref[...], feat2, 0, 0).astype(BF16)

    with jax.named_scope("barrier"):
        pl.semaphore_wait(barrier, 70)

    def send_boundary(src, dst, k, *distances):
        def one(r):
            peer = dom_peer(r)
            remote(src.at[part(peer, 16)], dst.at[part(dom, 16)], a2a_send.at[k], a2a_recv.at[k],
                   {"dom": peer}).start()
        for first, last, step in distances:
            loop(0, (last - first) // step, lambda i: one(first + step * i))

    def keep_boundary(src, dst):
        dst[part(dom, 16), :] = src[part(dom, 16), :]

    def wait_boundary(dst, k):
        wait(dst.at[pl.ds(0, 63 * 16)], a2a_recv.at[k])

    with jax.named_scope("send_rows"):
        send_boundary(out_ref, halo_ref, 0, (1, 64, 1))
        keep_boundary(out_ref, halo_ref)

    with jax.named_scope("adjacency"):
        loads[3].wait()
        nb = nb_ref[...]
        entry = nb - 128
        place_of = (
            lax.shift_left(lax.shift_right_arithmetic(entry, 3), 4) + jnp.bitwise_and(entry, 7))
        row_ids = iota((1024, 128), 0)
        count = jnp.zeros((1024, 128), F32)
        for k in range(8, 16):
            count = count + jnp.where(row_ids == place_of[k:k + 1, :], 1.0, 0.0)
        lower = count.T
        adjt_ref[:, 0:128] = count.astype(BF16)
        adjt_ref[:, 128:256] = pltpu.roll(count, 8, 0).astype(BF16)
        adj_ref[0:128, :] = lower.astype(BF16)
        adj_ref[128:256, :] = pltpu.roll(lower, 8, 1).astype(BF16)
        own_ids = iota((128, 128), 0)
        own_t = jnp.zeros((128, 128), F32)
        for k in range(8):
            own_t = own_t + jnp.where(own_ids == nb[k:k + 1, :], 1.0, 0.0)
        own_adj = own_t.T.astype(BF16)
        own_adj_t = own_t.astype(BF16)
        own_sum = dot(own_adj, feat)
        lt_ref[0] = feat.astype(F32).T.astype(BF16)
        for load in loads[4:]:
            load.wait()
        pre_self = dot(feat, ws_ref[...])

    with jax.named_scope("wait_rows"):
        wait_boundary(halo_ref, 0)
    with jax.named_scope("grad_pre"):
        halo_sum = dot(adj_ref[...], halo_ref[...])
        summed = own_sum + jnp.concatenate([halo_sum[0:128], halo_sum[128:256]], axis=1)
        agg = (summed * (1.0 / 16.0)).astype(BF16)
        pre = pre_self + dot(agg, wn_ref[...])
        grad_pre = (cot_ref[...].astype(F32) * gelu_slope(pre)).astype(BF16)

    with jax.named_scope("weight_grads"):
        lt_ref[1] = agg.astype(F32).T.astype(BF16)
        scale = 65536.0 ** -0.5
        pair_out[...] = (dot(lt_ref[other], grad_pre) * scale).astype(BF16)
        for r in range(4):
            i = lax.rem(x + 1 + r, 4)
            remote(pair_out.at[part(i, 128)], pair_in.at[part(i, 128)], pair_send.at[i],
                   pair_recv.at[i], sibling).start()
        own_ref[...] = dot(lt_ref[core], grad_pre) * scale

    with jax.named_scope("boundary_grads"):
        grad_agg = (dot(grad_pre, wn_ref[...], 1, 1) * (1.0 / 16.0)).astype(BF16)
        grad_agg2 = jnp.concatenate([grad_agg[:, :256], grad_agg[:, 256:]], axis=0)
        back_ref[...] = dot(adjt_ref[...], grad_agg2).astype(BF16)

    def send_one(s, i):
        first, width, (n, me, at), _, _ = strips[s]
        rows = part(i, 512 // n)
        cols = pl.ds(first, width)
        one_out[s][rows, :] = (
            own_ref[rows, cols] + pair_in[rows, cols].astype(F32)).astype(BF16)

        @pl.when(i != me)
        def _():
            remote(one_out[s].at[rows], one_in[s].at[part(me, 512 // n)], one_send.at[s],
                   one_recv.at[s], at(i)).start()

    with jax.named_scope("step_one"):
        for r in range(4):
            i = lax.rem(x + 1 + r, 4)
            wait(pair_in.at[part(i, 128)], pair_recv.at[i])
            for s, (_, _, (n1, _, _), _, _) in enumerate(strips):
                for j in range(n1 // 4):
                    send_one(s, n1 // 4 * i + j)

    with jax.named_scope("send_grads"):
        send_boundary(back_ref, ret_ref, 1, *BATCHES[0])
        keep_boundary(back_ref, ret_ref)
    with jax.named_scope("base"):
        base_ref[...] = dot(grad_pre, ws_ref[...], 1, 1) + dot(own_adj_t, grad_agg)

    for s, (first, width, (n1, me1, _), (n2, me2, at2), _) in enumerate(strips):
        with jax.named_scope("step_two_%d" % s):
            rows1 = 512 // n1
            mine = part(me1, rows1)
            cols = pl.ds(first, width)
            total = own_ref[mine, cols] + pair_in[mine, cols].astype(F32)
            wait(one_in[s].at[pl.ds(0, 512 - rows1)], one_recv.at[s])
            for r in range(1, n1):
                total = total + one_in[s][part(lax.rem(me1 + r, n1), rows1), :].astype(F32)
            sum_ref[s][...] = total
            two_out[s][...] = total.astype(BF16)
            for r in range(1, n2):
                i = lax.rem(me2 + r, n2)
                remote(two_out[s].at[part(i, 16)], two_in[s].at[part(me2, 16)], two_send.at[s],
                       two_recv.at[s], at2(i)).start()
            if s == 0:
                send_boundary(back_ref, ret_ref, 1, *BATCHES[1])

    send_boundary(back_ref, ret_ref, 1, *BATCHES[2])

    for s, (_, _, _, (n2, me2, _), (n3, me3, at3)) in enumerate(strips):
        with jax.named_scope("step_three_%d" % s):
            small = sum_ref[s][part(me2, 16), :]
            wait(two_in[s].at[pl.ds(0, 16 * (n2 - 1))], two_recv.at[s])
            for r in range(1, n2):
                small = small + two_in[s][part(lax.rem(me2 + r, n2), 16), :].astype(F32)
            three_ref[s][part(me3, 16), :] = small.astype(BF16)
            for r in range(1, n3):
                here = three_ref[s].at[part(me3, 16)]
                remote(here, here, three_send.at[s], three_recv.at[s],
                       at3(lax.rem(me3 + r, n3))).start()

    send_boundary(back_ref, ret_ref, 1, *BATCHES[3])

    def final(s, rows, count):
        first, width = strips[s][:2]
        return gw_ref.at[core, pl.ds(rows, count), pl.ds(first, width)]

    for s, (first, width, (n1, me1, _), (n2, me2, at2), (n3, _, _)) in enumerate(strips):
        with jax.named_scope("gather_one_%d" % s):
            wait(three_ref[s].at[pl.ds(0, 16 * (n3 - 1))], three_recv.at[s])
            done = three_ref[s][0:16, :].astype(F32)
            for i in range(1, n3):
                done = done + three_ref[s][16 * i:16 * i + 16, :].astype(F32)
            row = pl.multiple_of(me1 * (512 // n1) + me2 * 16, 16)
            gw_ref[core, pl.ds(row, 16), pl.ds(first, width)] = done.astype(BF16)
            for r in range(1, n2):
                remote(final(s, row, 16), final(s, row, 16), ag1_send.at[s], ag1_recv.at[s],
                       at2(lax.rem(me2 + r, n2))).start()

    send_boundary(back_ref, ret_ref, 1, *BATCHES[4])

    def forward(s, unit, row, count):
        remote(final(s, row, count), final(s, row, count), fin_send.at[s, unit],
               fin_recv.at[s, unit], sibling).start()

    for s, (_, _, (n1, me1, at1), (n2, _, _), _) in enumerate(strips):
        with jax.named_scope("gather_two_%d" % s):
            rows1 = 512 // n1
            wait(final(s, 0, 16 * (n2 - 1)), ag1_recv.at[s])
            row = pl.multiple_of(me1 * rows1, rows1)
            for r in range(1, n1):
                unit = me1 if n1 == 4 else 0
                remote(final(s, row, rows1), final(s, row, rows1), ag2_send.at[s],
                       ag2_recv.at[s, unit], at1(lax.rem(me1 + r, n1))).start()
            if n1 == 4:
                forward(s, me1, row, rows1)
    send_boundary(back_ref, ret_ref, 1, *BATCHES[5])

    with jax.named_scope("forward"):
        for s, (_, _, (n1, me1, _), _, _) in enumerate(strips):
            if n1 == 4:
                for r in range(1, 4):
                    i = lax.rem(me1 + r, 4)
                    row = pl.multiple_of(i * 128, 128)
                    wait(final(s, row, 128), ag2_recv.at[s, i])
                    forward(s, i, row, 128)
            else:
                wait(final(s, 0, 448), ag2_recv.at[s, 0])
                forward(s, 0, 0, 512)

    with jax.named_scope("wait_grads"):
        wait_boundary(ret_ref, 1)
    with jax.named_scope("feature_grads"):
        returned = dot(sel_ref[...], ret_ref[...])
        gfeat_ref[...] = (
            base_ref[...] + jnp.concatenate([returned[0:128], returned[128:256]], axis=1)
        ).astype(BF16)

    with jax.named_scope("finish"):
        wait(out_ref.at[pl.ds(0, 63 * 16)], a2a_send.at[0])
        wait(back_ref.at[pl.ds(0, 63 * 16)], a2a_send.at[1])
        for i in range(4):
            wait(pair_out.at[pl.ds(128 * i, 128)], pair_send.at[i])
        for s, (_, _, (n1, _, _), (n2, _, _), (n3, _, _)) in enumerate(strips):
            rows1 = 512 // n1
            wait(one_out[s].at[pl.ds(0, 512 - rows1)], one_send.at[s])
            wait(two_out[s].at[pl.ds(0, 16 * (n2 - 1))], two_send.at[s])
            wait(three_ref[s].at[pl.ds(0, 16 * (n3 - 1))], three_send.at[s])
            wait(final(s, 0, 16 * (n2 - 1)), ag1_send.at[s])
            wait(final(s, 0, 512 - rows1), ag2_send.at[s])
            units = 4 if n1 == 4 else 1
            for unit in range(units):
                wait(final(s, 0, 512 // units), fin_send.at[s, unit])
                wait(final(s, 0, 512 // units), fin_recv.at[s, unit])


def write_kernel(gfeat_in, gw_in, gfeat_ref, gws_ref, gwn_ref, wide_ref, sem):
    copies = [pltpu.make_async_copy(gfeat_in, gfeat_ref, sem.at[0])]
    copies[0].start()
    for c, ref in enumerate((gws_ref, gwn_ref)):
        for half in range(2):
            rows = pl.ds(256 * half, 256)
            wide_ref[c, rows, :] = gw_in[c, rows, :].astype(F32)
            copy = pltpu.make_async_copy(
                wide_ref.at[c, rows], ref.at[rows], sem.at[1 + 2 * c + half])
            copy.start()
            copies.append(copy)
    for copy in copies:
        copy.wait()


def strip_scratch(shape, dtype):
    return tuple(
        pltpu.VMEM(shape(width, 4 if order[0] == "x" else 8), dtype) for _, width, order in STRIPS
    )


def local(features, w_self, w_neigh, cotangent, neighbors, send_rows, send_count):
    vmem = pl.BlockSpec(memory_space=pltpu.VMEM)
    hbm = pl.BlockSpec(memory_space=pltpu.HBM)
    dma = pltpu.SemaphoreType.DMA
    grad_features, grads = pl.pallas_call(
        kernel,
        out_shape=(
            pltpu.VMEM((128, 512), BF16),
            pltpu.VMEM((2, 512, 512), BF16),
        ),
        in_specs=[hbm] * 7,
        out_specs=(vmem, vmem),
        scratch_shapes=[
            pltpu.VMEM((128, 512), BF16),
            pltpu.VMEM((512, 512), BF16),
            pltpu.VMEM((512, 512), BF16),
            pltpu.VMEM((128, 512), BF16),
            pltpu.VMEM((16, 128), jnp.int32),
            pltpu.VMEM((8, 64), jnp.int32),
            pltpu.VMEM((1, 64), jnp.int32),
            pltpu.VMEM((256, 1024), BF16),
            pltpu.VMEM((256, 1024), BF16),
            pltpu.VMEM((1024, 256), BF16),
            pltpu.VMEM((1024, 256), BF16),
            pltpu.VMEM((1024, 256), BF16),
            pltpu.VMEM((1024, 256), BF16),
            pltpu.VMEM((1024, 256), BF16),
            pltpu.VMEM((2, 512, 128), BF16),
            pltpu.VMEM((512, 512), F32),
            pltpu.VMEM((512, 512), BF16),
            pltpu.VMEM((512, 512), BF16),
            strip_scratch(lambda w, n: (512, w), BF16),
            strip_scratch(lambda w, n: (512, w), BF16),
            strip_scratch(lambda w, n: (512 // n, w), F32),
            strip_scratch(lambda w, n: (512 // n, w), BF16),
            strip_scratch(lambda w, n: (512 // n, w), BF16),
            strip_scratch(lambda w, n: (128, w), BF16),
            pltpu.VMEM((128, 512), F32),
            dma((7,)), dma((2,)), dma((2,)), dma((4,)), dma((4,)),
            *([dma((len(STRIPS),))] * 9), *([dma((len(STRIPS), 4))] * 3),
        ],
        compiler_params=pltpu.CompilerParams(
            collective_id=0, has_side_effects=True, vmem_limit_bytes=40 << 20
        ),
        name="sage_backward",
    )(*(
        pltpu.with_memory_space_constraint(array, pltpu.HBM)
        for array in (
            features, w_self, w_neigh, cotangent, neighbors.T,
            send_rows.reshape(64, 8).T, send_count.reshape(1, 64),
        )
    ))
    return pl.pallas_call(
        write_kernel,
        out_shape=(
            jax.ShapeDtypeStruct((128, 512), BF16),
            jax.ShapeDtypeStruct((512, 512), F32),
            jax.ShapeDtypeStruct((512, 512), F32),
        ),
        in_specs=[vmem, vmem],
        out_specs=(hbm, hbm, hbm),
        scratch_shapes=[pltpu.VMEM((2, 512, 512), F32), dma((5,))],
        compiler_params=pltpu.CompilerParams(vmem_limit_bytes=8 << 20),
        name="write_results",
    )(grad_features, grads)


def solution(mesh):
    placed = (
        P(("grp", "dom"), None),
        P(),
        P(),
        P(("grp", "dom"), None),
        P(("grp", "dom"), None),
        P("grp", "dom", None, None),
        P("grp", "dom", None),
    )
    return jax.shard_map(
        local,
        mesh=mesh,
        in_specs=placed,
        out_specs=(P(("grp", "dom"), None), P(), P()),
        check_vma=False,
    )
```

```python
import functools

import jax
import jax.numpy as jnp
from jax import lax
from jax.experimental import pallas as pl
from jax.experimental.pallas import tpu as pltpu
from jax.sharding import PartitionSpec as P

MESH = pl.DeviceIdType.MESH
F32 = jnp.float32
BF16 = jnp.bfloat16


STRIPS = ((0, 256, "xzy"), (256, 128, "zxy"), (384, 128, "yxz"))
BATCHES = ((), ((0, 31),), (), (), ((31, 63),), ())


def dot(left, right, left_dim=1, right_dim=0):
    return lax.dot_general(
        left, right, (((left_dim,), (right_dim,)), ((), ())), preferred_element_type=F32
    )


def iota(shape, dim):
    return lax.broadcasted_iota(jnp.int32, shape, dim)


def gelu_slope(v):
    root = 0.7978845608028654
    square = v * v
    t = jnp.tanh(root * (v + 0.044715 * square * v))
    return 0.5 * (1.0 + t) + (0.5 * root) * v * (1.0 - t * t) * (1.0 + 0.134145 * square)


def kernel(
    feat_hbm, ws_hbm, wn_hbm, cot_hbm, nb_hbm, rows_hbm, count_hbm,
    gfeat_ref, gw_ref,
    feat_ref, w_ref, cot_ref, nb_ref, rows_ref, count_ref,
    sel_ref, adj_ref, adjt_ref, out_ref, halo_ref, back_ref, ret_ref,
    lt_ref, lt_pair, gp_ref, own_ref, one_out, one_in, sum_ref, two_out, two_in, three_ref, base_ref,
    all_sent_ref, load_sem, sent, a2a_recv, pair_recv, one_recv, two_recv, three_recv, ag1_recv,
    ag2_recv, fin_recv,
):
    grp = lax.axis_index("grp")
    dom = lax.axis_index("dom")
    core = lax.rem(dom, 2)
    other = 1 - core
    sibling = {"dom": dom + 1 - 2 * core}
    y = lax.rem(dom // 2, 8)
    x = dom // 16

    axis_x = (4, x, lambda i: {"dom": i * 16 + y * 2 + core})
    axis_y = (8, y, lambda i: {"dom": x * 16 + i * 2 + core})
    axis_z = (8, grp, lambda i: {"grp": i})
    axes = {"x": axis_x, "y": axis_y, "z": axis_z}
    strips = tuple(
        (first, width) + tuple(axes[name] for name in order) for first, width, order in STRIPS
    )

    def dom_peer(r):
        return lax.rem(dom + r, 64)

    def far_peer(q):
        i = lax.rem(q, 8)
        dy = 4 + (i + 1) // 2 * (1 - 2 * lax.rem(i, 2))
        o = 7 - q // 8
        return (
            lax.rem(x + o // 2, 4) * 16 + lax.rem(y + dy, 8) * 2 + lax.rem(core + lax.rem(o, 2), 2))

    def loop(first, last, body):
        lax.fori_loop(first, last, lambda i, c: (body(i), c)[1], 0)

    def remote(src, dst, recv, device):
        return pltpu.make_async_remote_copy(
            src_ref=src, dst_ref=dst, send_sem=sent, recv_sem=recv,
            device_id=device, device_id_type=MESH,
        )

    def wait(ref, sem):
        pltpu.make_async_copy(ref, ref, sem).wait()

    def part(i, size):
        return pl.ds(pl.multiple_of(i * size, size), size)

    loads = [
        pltpu.make_async_copy(src, dst, load_sem.at[i])
        for i, src, dst in [
            (0, rows_hbm, rows_ref), (1, count_hbm, count_ref), (2, feat_hbm, feat_ref),
            (3, nb_hbm, nb_ref), (4, cot_hbm, cot_ref),
            (5, ws_hbm, w_ref.at[0]), (5, wn_hbm, w_ref.at[1]),
        ]
    ]
    for load in loads:
        load.start()

    barrier = pltpu.get_barrier_semaphore()
    with jax.named_scope("greet"):
        loop(1, 64, lambda r: pl.semaphore_signal(
            barrier, inc=1, device_id={"dom": dom_peer(r)}, device_id_type=MESH))
        loop(1, 8, lambda r: pl.semaphore_signal(
            barrier, inc=1, device_id={"grp": lax.rem(grp + r, 8)}, device_id_type=MESH))

    with jax.named_scope("outgoing"):
        col = iota((1, 1024), 1)
        slot_of = jnp.bitwise_and(col, 7)
        half_of = jnp.bitwise_and(lax.shift_right_logical(col, 3), 1)
        in_peer = (iota((64, 1024), 0) == lax.shift_right_logical(col, 4)).astype(BF16)
        for load in loads[:3]:
            load.wait()
        counts = jnp.broadcast_to(count_ref[...], (8, 64))
        table = jnp.concatenate([rows_ref[...], counts], axis=0).astype(F32).astype(BF16)
        spread = dot(table, in_peer)
        row = jnp.sum(
            jnp.where(iota((8, 1024), 0) == slot_of, spread[0:8], 0.0), axis=0, keepdims=True)
        live = spread[8:9] > slot_of.astype(F32)
        target = jnp.where(live, row + 128.0 * half_of.astype(F32), 512.0)
        sel_ref[...] = (iota((256, 1024), 0).astype(F32) == target).astype(BF16)
        feat = feat_ref[...]
        feat2 = jnp.concatenate([feat[:, :256], feat[:, 256:]], axis=0)
        out_ref[...] = dot(sel_ref[...], feat2, 0, 0).astype(BF16)

    with jax.named_scope("barrier"):
        pl.semaphore_wait(barrier, 70)

    def send_boundary(src, dst, k, *distances):
        def one(r):
            peer = far_peer(r) if k == 0 else dom_peer(r + 1)
            remote(src.at[part(peer, 16)], dst.at[part(dom, 16)], a2a_recv.at[k],
                   {"dom": peer}).start()
        for first, last in distances:
            loop(first, last, one)

    def keep_boundary(src, dst):
        dst[part(dom, 16), :] = src[part(dom, 16), :]

    def wait_boundary(dst, k):
        wait(dst.at[pl.ds(0, 63 * 16)], a2a_recv.at[k])

    with jax.named_scope("send_rows"):
        send_boundary(out_ref, halo_ref, 0, (0, 63))
        keep_boundary(out_ref, halo_ref)

    with jax.named_scope("adjacency"):
        loads[3].wait()
        nb = nb_ref[...]
        entry = nb - 128
        place_of = (
            lax.shift_left(lax.shift_right_arithmetic(entry, 3), 4) + jnp.bitwise_and(entry, 7))
        row_ids = iota((1024, 128), 0)
        count = jnp.zeros((1024, 128), F32)
        for k in range(8, 16):
            count = count + jnp.where(row_ids == place_of[k:k + 1, :], 1.0, 0.0)
        lower = count.T
        adjt_ref[:, 0:128] = count.astype(BF16)
        adjt_ref[:, 128:256] = pltpu.roll(count, 8, 0).astype(BF16)
        adj_ref[0:128, :] = lower.astype(BF16)
        adj_ref[128:256, :] = pltpu.roll(lower, 8, 1).astype(BF16)
        own_ids = iota((128, 128), 0)
        own_t = jnp.zeros((128, 128), F32)
        for k in range(8):
            own_t = own_t + jnp.where(own_ids == nb[k:k + 1, :], 1.0, 0.0)
        own_adj = own_t.T.astype(BF16)
        own_adj_t = own_t.astype(BF16)
        own_sum = dot(own_adj, feat)
        lt_ref[0] = feat.astype(F32).T.astype(BF16)
        loads[4].wait()
        wait(w_ref, load_sem.at[5])
        pre_self = dot(feat, w_ref[0])

    with jax.named_scope("wait_rows"):
        wait_boundary(halo_ref, 0)
    with jax.named_scope("grad_pre"):
        halo_sum = dot(adj_ref[...], halo_ref[...])
        summed = own_sum + jnp.concatenate([halo_sum[0:128], halo_sum[128:256]], axis=1)
        agg = (summed * (1.0 / 16.0)).astype(BF16)
        lt_ref[1] = agg.astype(F32).T.astype(BF16)
        remote(lt_ref.at[other], lt_pair, pair_recv.at[0], sibling).start()
        pre = pre_self + dot(agg, w_ref[1])
        grad_pre = (cot_ref[...].astype(F32) * gelu_slope(pre)).astype(BF16)
        gp_ref[0:128, :] = grad_pre
        remote(gp_ref.at[pl.ds(0, 128)], gp_ref.at[pl.ds(128, 128)], pair_recv.at[1],
               sibling).start()

    with jax.named_scope("boundary_grads"):
        grad_agg = (dot(grad_pre, w_ref[1], 1, 1) * (1.0 / 16.0)).astype(BF16)
        grad_agg2 = jnp.concatenate([grad_agg[:, :256], grad_agg[:, 256:]], axis=0)
        back_ref[...] = dot(adjt_ref[...], grad_agg2).astype(BF16)

    def send_one(s, i):
        first, width, (n, me, at), _, _ = strips[s]
        rows = part(i, 512 // n)
        one_out[s][rows, :] = own_ref[rows, pl.ds(first, width)].astype(BF16)

        @pl.when(i != me)
        def _():
            remote(one_out[s].at[rows], one_in[s].at[part(me, 512 // n)], one_recv.at[s],
                   at(i)).start()

    with jax.named_scope("step_one"):
        wait(lt_pair, pair_recv.at[0])
        wait(gp_ref.at[pl.ds(0, 128)], pair_recv.at[1])
        both = gp_ref[...]
        scale = 65536.0 ** -0.5
        for r in range(4):
            i = lax.rem(x + 1 + r, 4)
            rows = part(i, 128)
            left = jnp.concatenate([lt_ref[core, rows, :], lt_pair[rows, :]], axis=1)
            own_ref[rows, :] = dot(left, both) * scale
            for s, (_, _, (n1, _, _), _, _) in enumerate(strips):
                if n1 == 8 or r < 3:
                    for j in range(n1 // 4):
                        send_one(s, n1 // 4 * i + j)

    with jax.named_scope("send_grads"):
        send_boundary(back_ref, ret_ref, 1, *BATCHES[0])
        keep_boundary(back_ref, ret_ref)
    with jax.named_scope("base"):
        base_ref[...] = dot(grad_pre, w_ref[0], 1, 1) + dot(own_adj_t, grad_agg)

    for s, (first, width, (n1, me1, _), (n2, me2, at2), _) in enumerate(strips):
        with jax.named_scope("step_two_%d" % s):
            rows1 = 512 // n1
            mine = part(me1, rows1)
            cols = pl.ds(first, width)
            total = own_ref[mine, cols]
            wait(one_in[s].at[pl.ds(0, 512 - rows1)], one_recv.at[s])
            for r in range(1, n1):
                total = total + one_in[s][part(lax.rem(me1 + r, n1), rows1), :].astype(F32)
            sum_ref[s][...] = total
            two_out[s][...] = total.astype(BF16)
            for r in range(1, n2):
                i = lax.rem(me2 + r, n2)
                remote(two_out[s].at[part(i, 16)], two_in[s].at[part(me2, 16)],
                       two_recv.at[s], at2(i)).start()
            if s == 0:
                send_boundary(back_ref, ret_ref, 1, *BATCHES[1])

    send_boundary(back_ref, ret_ref, 1, *BATCHES[2])

    for s, (_, _, _, (n2, me2, _), (n3, me3, at3)) in enumerate(strips):
        with jax.named_scope("step_three_%d" % s):
            small = sum_ref[s][part(me2, 16), :]
            wait(two_in[s].at[pl.ds(0, 16 * (n2 - 1))], two_recv.at[s])
            for r in range(1, n2):
                small = small + two_in[s][part(lax.rem(me2 + r, n2), 16), :].astype(F32)
            three_ref[s][part(me3, 16), :] = small.astype(BF16)
            for r in range(1, n3):
                here = three_ref[s].at[part(me3, 16)]
                remote(here, here, three_recv.at[s],
                       at3(lax.rem(me3 + r, n3))).start()

    send_boundary(back_ref, ret_ref, 1, *BATCHES[3])

    def final(s, rows, count):
        first, width = strips[s][:2]
        return gw_ref.at[core, pl.ds(rows, count), pl.ds(first, width)]

    for s, (first, width, (n1, me1, _), (n2, me2, at2), (n3, _, _)) in enumerate(strips):
        with jax.named_scope("gather_one_%d" % s):
            wait(three_ref[s].at[pl.ds(0, 16 * (n3 - 1))], three_recv.at[s])
            done = three_ref[s][0:16, :].astype(F32)
            for i in range(1, n3):
                done = done + three_ref[s][16 * i:16 * i + 16, :].astype(F32)
            row = pl.multiple_of(me1 * (512 // n1) + me2 * 16, 16)
            gw_ref[core, pl.ds(row, 16), pl.ds(first, width)] = done.astype(BF16)
            for r in range(1, n2):
                remote(final(s, row, 16), final(s, row, 16), ag1_recv.at[s],
                       at2(lax.rem(me2 + r, n2))).start()

    send_boundary(back_ref, ret_ref, 1, *BATCHES[4])

    def forward(s, row, count):
        remote(final(s, row, count), final(s, row, count), fin_recv, sibling).start()

    units = []
    for s, (_, _, (n1, _, _), _, _) in enumerate(strips):
        units.append(units[-1] + (4 if strips[s - 1][2][0] == 4 else 1) if s else 0)

    for s, (_, _, (n1, me1, at1), (n2, _, _), _) in enumerate(strips):
        with jax.named_scope("gather_two_%d" % s):
            rows1 = 512 // n1
            wait(final(s, 0, 16 * (n2 - 1)), ag1_recv.at[s])
            row = pl.multiple_of(me1 * rows1, rows1)
            for r in range(1, n1):
                unit = units[s] + me1 if n1 == 4 else units[s]
                remote(final(s, row, rows1), final(s, row, rows1), ag2_recv.at[unit],
                       at1(lax.rem(me1 + r, n1))).start()
            if n1 == 4:
                forward(s, row, rows1)

    send_boundary(back_ref, ret_ref, 1, *BATCHES[5])

    with jax.named_scope("forward"):
        for s, (_, _, (n1, me1, _), _, _) in enumerate(strips):
            if n1 == 4:
                for r in range(1, 4):
                    i = lax.rem(me1 + r, 4)
                    row = pl.multiple_of(i * 128, 128)
                    wait(final(s, row, 128), ag2_recv.at[units[s] + i])
                    forward(s, row, 128)
            else:
                wait(final(s, 0, 448), ag2_recv.at[units[s]])
                forward(s, 0, 512)

    with jax.named_scope("wait_grads"):
        wait_boundary(ret_ref, 1)
    with jax.named_scope("feature_grads"):
        returned = dot(sel_ref[...], ret_ref[...])
        gfeat_ref[...] = (
            base_ref[...] + jnp.concatenate([returned[0:128], returned[128:256]], axis=1)
        ).astype(BF16)

    with jax.named_scope("finish"):
        wait(all_sent_ref, sent)
        wait(gw_ref.at[other], fin_recv)


def write_kernel(gfeat_in, gw_in, gfeat_ref, gws_ref, gwn_ref, wide_ref, sem):
    copies = [pltpu.make_async_copy(gfeat_in, gfeat_ref, sem.at[0])]
    copies[0].start()
    for c, ref in enumerate((gws_ref, gwn_ref)):
        for half in range(2):
            rows = pl.ds(256 * half, 256)
            wide_ref[c, rows, :] = gw_in[c, rows, :].astype(F32)
            copy = pltpu.make_async_copy(
                wide_ref.at[c, rows], ref.at[rows], sem.at[1 + 2 * c + half])
            copy.start()
            copies.append(copy)
    for copy in copies:
        copy.wait()


def strip_scratch(shape, dtype):
    return tuple(
        pltpu.VMEM(shape(width, 4 if order[0] == "x" else 8), dtype) for _, width, order in STRIPS
    )


def sent_rows():
    length = {"x": 4, "y": 8, "z": 8}
    rows = 2 * 63 * 8 + 2 * 128 + 512
    for _, width, order in STRIPS:
        n1, n2, n3 = (length[axis] for axis in order)
        steps = 2 * (512 - 512 // n1) + 2 * 16 * (n2 - 1) + 16 * (n3 - 1)
        rows += steps * width // 512
    return rows


def local(features, w_self, w_neigh, cotangent, neighbors, send_rows, send_count):
    vmem = pl.BlockSpec(memory_space=pltpu.VMEM)
    hbm = pl.BlockSpec(memory_space=pltpu.HBM)
    dma = pltpu.SemaphoreType.DMA
    grad_features, grads = pl.pallas_call(
        kernel,
        out_shape=(
            pltpu.VMEM((128, 512), BF16),
            pltpu.VMEM((2, 512, 512), BF16),
        ),
        in_specs=[hbm] * 7,
        out_specs=(vmem, vmem),
        scratch_shapes=[
            pltpu.VMEM((128, 512), BF16),
            pltpu.VMEM((2, 512, 512), BF16),
            pltpu.VMEM((128, 512), BF16),
            pltpu.VMEM((16, 128), jnp.int32),
            pltpu.VMEM((8, 64), jnp.int32),
            pltpu.VMEM((1, 64), jnp.int32),
            pltpu.VMEM((256, 1024), BF16),
            pltpu.VMEM((256, 1024), BF16),
            pltpu.VMEM((1024, 256), BF16),
            pltpu.VMEM((1024, 256), BF16),
            pltpu.VMEM((1024, 256), BF16),
            pltpu.VMEM((1024, 256), BF16),
            pltpu.VMEM((1024, 256), BF16),
            pltpu.VMEM((2, 512, 128), BF16),
            pltpu.VMEM((512, 128), BF16),
            pltpu.VMEM((256, 512), BF16),
            pltpu.VMEM((512, 512), F32),
            strip_scratch(lambda w, n: (512, w), BF16),
            strip_scratch(lambda w, n: (512, w), BF16),
            strip_scratch(lambda w, n: (512 // n, w), F32),
            strip_scratch(lambda w, n: (512 // n, w), BF16),
            strip_scratch(lambda w, n: (512 // n, w), BF16),
            strip_scratch(lambda w, n: (128, w), BF16),
            pltpu.VMEM((128, 512), F32),
            pltpu.VMEM((sent_rows(), 512), BF16),
            dma((6,)), dma, dma((2,)), dma((2,)), *([dma((len(STRIPS),))] * 4),
            dma((sum(4 if order[0] == "x" else 1 for _, _, order in STRIPS),)), dma,
        ],
        compiler_params=pltpu.CompilerParams(
            collective_id=0, has_side_effects=True, vmem_limit_bytes=40 << 20
        ),
        name="sage_backward",
    )(*(
        pltpu.with_memory_space_constraint(array, pltpu.HBM)
        for array in (
            features, w_self, w_neigh, cotangent, neighbors.T,
            send_rows.reshape(64, 8).T, send_count.reshape(1, 64),
        )
    ))
    return pl.pallas_call(
        write_kernel,
        out_shape=(
            jax.ShapeDtypeStruct((128, 512), BF16),
            jax.ShapeDtypeStruct((512, 512), F32),
            jax.ShapeDtypeStruct((512, 512), F32),
        ),
        in_specs=[vmem, vmem],
        out_specs=(hbm, hbm, hbm),
        scratch_shapes=[pltpu.VMEM((2, 512, 512), F32), dma((5,))],
        compiler_params=pltpu.CompilerParams(vmem_limit_bytes=8 << 20),
        name="write_results",
    )(grad_features, grads)


def solution(mesh):
    placed = (
        P(("grp", "dom"), None),
        P(),
        P(),
        P(("grp", "dom"), None),
        P(("grp", "dom"), None),
        P("grp", "dom", None, None),
        P("grp", "dom", None),
    )
    return jax.shard_map(
        local,
        mesh=mesh,
        in_specs=placed,
        out_specs=(P(("grp", "dom"), None), P(), P()),
        check_vma=False,
    )
```

```python
import functools

import jax
import jax.numpy as jnp
from jax import lax
from jax.experimental import pallas as pl
from jax.experimental.pallas import tpu as pltpu
from jax.sharding import PartitionSpec as P

MESH = pl.DeviceIdType.MESH
F32 = jnp.float32
BF16 = jnp.bfloat16


STRIPS = ((0, 256, "xzy"), (256, 128, "zxy"), (384, 128, "yxz"))
BATCHES = (((0, 15),), ((15, 31),), (), ((31, 47),), ((47, 63),), ())


def dot(left, right, left_dim=1, right_dim=0):
    return lax.dot_general(
        left, right, (((left_dim,), (right_dim,)), ((), ())), preferred_element_type=F32
    )


def iota(shape, dim):
    return lax.broadcasted_iota(jnp.int32, shape, dim)


def gelu_slope(v):
    root = 0.7978845608028654
    square = v * v
    t = jnp.tanh(root * (v + 0.044715 * square * v))
    return 0.5 * (1.0 + t) + (0.5 * root) * v * (1.0 - t * t) * (1.0 + 0.134145 * square)


def kernel(
    feat_hbm, ws_hbm, wn_hbm, cot_hbm, nb_hbm, rows_hbm, count_hbm,
    gfeat_ref, gw_ref,
    feat_ref, w_ref, cot_ref, nb_ref, rows_ref, count_ref,
    sel_ref, adj_ref, adjt_ref, out_ref, halo_ref, back_ref, ret_ref,
    lt_ref, lt_pair, gp_ref, own_ref, one_out, one_in, sum_ref, two_out, two_in, three_ref, base_ref,
    all_sent_ref, load_sem, sent, a2a_recv, pair_recv, one_recv, two_recv, three_recv, ag1_recv,
    ag2_recv, fin_recv,
):
    grp = lax.axis_index("grp")
    dom = lax.axis_index("dom")
    core = lax.rem(dom, 2)
    other = 1 - core
    sibling = {"dom": dom + 1 - 2 * core}
    y = lax.rem(dom // 2, 8)
    x = dom // 16

    axis_x = (4, x, lambda i: {"dom": i * 16 + y * 2 + core})
    axis_y = (8, y, lambda i: {"dom": x * 16 + i * 2 + core})
    axis_z = (8, grp, lambda i: {"grp": i})
    axes = {"x": axis_x, "y": axis_y, "z": axis_z}
    strips = tuple(
        (first, width) + tuple(axes[name] for name in order) for first, width, order in STRIPS
    )

    def dom_peer(r):
        return lax.rem(dom + r, 64)

    def far_peer(q):
        i = lax.rem(q, 8)
        dy = 4 + (i + 1) // 2 * (1 - 2 * lax.rem(i, 2))
        o = 7 - q // 8
        return (
            lax.rem(x + o // 2, 4) * 16 + lax.rem(y + dy, 8) * 2 + lax.rem(core + lax.rem(o, 2), 2))

    def loop(first, last, body):
        lax.fori_loop(first, last, lambda i, c: (body(i), c)[1], 0)

    def remote(src, dst, recv, device):
        return pltpu.make_async_remote_copy(
            src_ref=src, dst_ref=dst, send_sem=sent, recv_sem=recv,
            device_id=device, device_id_type=MESH,
        )

    def wait(ref, sem):
        pltpu.make_async_copy(ref, ref, sem).wait()

    def part(i, size):
        return pl.ds(pl.multiple_of(i * size, size), size)

    loads = [
        pltpu.make_async_copy(src, dst, load_sem.at[i])
        for i, src, dst in [
            (0, rows_hbm, rows_ref), (1, count_hbm, count_ref), (2, feat_hbm, feat_ref),
            (3, nb_hbm, nb_ref), (4, cot_hbm, cot_ref),
            (5, ws_hbm, w_ref.at[0]), (5, wn_hbm, w_ref.at[1]),
        ]
    ]
    for load in loads:
        load.start()

    barrier = pltpu.get_barrier_semaphore()
    with jax.named_scope("greet"):
        loop(1, 64, lambda r: pl.semaphore_signal(
            barrier, inc=1, device_id={"dom": dom_peer(r)}, device_id_type=MESH))
        loop(1, 8, lambda r: pl.semaphore_signal(
            barrier, inc=1, device_id={"grp": lax.rem(grp + r, 8)}, device_id_type=MESH))

    with jax.named_scope("outgoing"):
        col = iota((1, 1024), 1)
        slot_of = jnp.bitwise_and(col, 7)
        half_of = jnp.bitwise_and(lax.shift_right_logical(col, 3), 1)
        in_peer = (iota((64, 1024), 0) == lax.shift_right_logical(col, 4)).astype(BF16)
        for load in loads[:3]:
            load.wait()
        counts = jnp.broadcast_to(count_ref[...], (8, 64))
        table = jnp.concatenate([rows_ref[...], counts], axis=0).astype(F32).astype(BF16)
        spread = dot(table, in_peer)
        row = jnp.sum(
            jnp.where(iota((8, 1024), 0) == slot_of, spread[0:8], 0.0), axis=0, keepdims=True)
        live = spread[8:9] > slot_of.astype(F32)
        target = jnp.where(live, row + 128.0 * half_of.astype(F32), 512.0)
        sel_ref[...] = (iota((256, 1024), 0).astype(F32) == target).astype(BF16)
        feat = feat_ref[...]
        feat2 = jnp.concatenate([feat[:, :256], feat[:, 256:]], axis=0)
        out_ref[...] = dot(sel_ref[...], feat2, 0, 0).astype(BF16)

    with jax.named_scope("barrier"):
        pl.semaphore_wait(barrier, 70)

    def send_boundary(src, dst, k, *distances):
        def one(r):
            peer = far_peer(r) if k == 0 else dom_peer(r + 1)
            remote(src.at[part(peer, 16)], dst.at[part(dom, 16)], a2a_recv.at[k],
                   {"dom": peer}).start()
        for first, last in distances:
            loop(first, last, one)

    def keep_boundary(src, dst):
        dst[part(dom, 16), :] = src[part(dom, 16), :]

    def wait_boundary(dst, k):
        wait(dst.at[pl.ds(0, 63 * 16)], a2a_recv.at[k])

    with jax.named_scope("send_rows"):
        send_boundary(out_ref, halo_ref, 0, (0, 63))
        keep_boundary(out_ref, halo_ref)

    with jax.named_scope("adjacency"):
        loads[3].wait()
        nb = nb_ref[...]
        entry = nb - 128
        place_of = (
            lax.shift_left(lax.shift_right_arithmetic(entry, 3), 4) + jnp.bitwise_and(entry, 7))
        row_ids = iota((1024, 128), 0)
        count = jnp.zeros((1024, 128), F32)
        for k in range(8, 16):
            count = count + jnp.where(row_ids == place_of[k:k + 1, :], 1.0, 0.0)
        lower = count.T
        adjt_ref[:, 0:128] = count.astype(BF16)
        adjt_ref[:, 128:256] = pltpu.roll(count, 8, 0).astype(BF16)
        adj_ref[0:128, :] = lower.astype(BF16)
        adj_ref[128:256, :] = pltpu.roll(lower, 8, 1).astype(BF16)
        own_ids = iota((128, 128), 0)
        own_t = jnp.zeros((128, 128), F32)
        for k in range(8):
            own_t = own_t + jnp.where(own_ids == nb[k:k + 1, :], 1.0, 0.0)
        own_adj = own_t.T.astype(BF16)
        own_adj_t = own_t.astype(BF16)
        own_sum = dot(own_adj, feat)
        lt_ref[0] = feat.astype(F32).T.astype(BF16)
        loads[4].wait()
        wait(w_ref, load_sem.at[5])
        pre_self = dot(feat, w_ref[0])

    with jax.named_scope("wait_rows"):
        wait_boundary(halo_ref, 0)
    with jax.named_scope("grad_pre"):
        halo_sum = dot(adj_ref[...], halo_ref[...])
        summed = own_sum + jnp.concatenate([halo_sum[0:128], halo_sum[128:256]], axis=1)
        agg = (summed * (1.0 / 16.0)).astype(BF16)
        lt_ref[1] = agg.astype(F32).T.astype(BF16)
        remote(lt_ref.at[other], lt_pair, pair_recv.at[0], sibling).start()
        pre = pre_self + dot(agg, w_ref[1])
        grad_pre = (cot_ref[...].astype(F32) * gelu_slope(pre)).astype(BF16)
        gp_ref[0:128, :] = grad_pre
        remote(gp_ref.at[pl.ds(0, 128)], gp_ref.at[pl.ds(128, 128)], pair_recv.at[1],
               sibling).start()

    with jax.named_scope("boundary_grads"):
        grad_agg = (dot(grad_pre, w_ref[1], 1, 1) * (1.0 / 16.0)).astype(BF16)
        grad_agg2 = jnp.concatenate([grad_agg[:, :256], grad_agg[:, 256:]], axis=0)
        back_ref[...] = dot(adjt_ref[...], grad_agg2).astype(BF16)

    def send_one(s, i):
        first, width, (n, me, at), _, _ = strips[s]
        rows = part(i, 512 // n)
        one_out[s][rows, :] = own_ref[rows, pl.ds(first, width)].astype(BF16)

        @pl.when(i != me)
        def _():
            remote(one_out[s].at[rows], one_in[s].at[part(me, 512 // n)], one_recv.at[s],
                   at(i)).start()

    with jax.named_scope("step_one"):
        wait(lt_pair, pair_recv.at[0])
        wait(gp_ref.at[pl.ds(0, 128)], pair_recv.at[1])
        both = gp_ref[...]
        scale = 65536.0 ** -0.5
        for r in range(4):
            i = lax.rem(x + 1 + r, 4)
            rows = part(i, 128)
            left = jnp.concatenate([lt_ref[core, rows, :], lt_pair[rows, :]], axis=1)
            own_ref[rows, :] = dot(left, both) * scale
            for s, (_, _, (n1, _, _), _, _) in enumerate(strips):
                if n1 == 8 or r < 3:
                    for j in range(n1 // 4):
                        send_one(s, n1 // 4 * i + j)

    with jax.named_scope("send_grads"):
        send_boundary(back_ref, ret_ref, 1, *BATCHES[0])
        keep_boundary(back_ref, ret_ref)
    with jax.named_scope("base"):
        base_ref[...] = dot(grad_pre, w_ref[0], 1, 1) + dot(own_adj_t, grad_agg)

    for s, (first, width, (n1, me1, _), (n2, me2, at2), _) in enumerate(strips):
        with jax.named_scope("step_two_%d" % s):
            rows1 = 512 // n1
            mine = part(me1, rows1)
            cols = pl.ds(first, width)
            total = own_ref[mine, cols]
            wait(one_in[s].at[pl.ds(0, 512 - rows1)], one_recv.at[s])
            for r in range(1, n1):
                total = total + one_in[s][part(lax.rem(me1 + r, n1), rows1), :].astype(F32)
            sum_ref[s][...] = total
            two_out[s][...] = total.astype(BF16)
            for r in range(1, n2):
                i = lax.rem(me2 + r, n2)
                remote(two_out[s].at[part(i, 16)], two_in[s].at[part(me2, 16)],
                       two_recv.at[s], at2(i)).start()
            if s == 0:
                send_boundary(back_ref, ret_ref, 1, *BATCHES[1])

    send_boundary(back_ref, ret_ref, 1, *BATCHES[2])

    for s in sorted(range(len(strips)), key=lambda s: strips[s][2][0] == 4):
        _, _, _, (n2, me2, _), (n3, me3, at3) = strips[s]
        with jax.named_scope("step_three_%d" % s):
            small = sum_ref[s][part(me2, 16), :]
            wait(two_in[s].at[pl.ds(0, 16 * (n2 - 1))], two_recv.at[s])
            for r in range(1, n2):
                small = small + two_in[s][part(lax.rem(me2 + r, n2), 16), :].astype(F32)
            three_ref[s][part(me3, 16), :] = small.astype(BF16)
            for r in range(1, n3):
                here = three_ref[s].at[part(me3, 16)]
                remote(here, here, three_recv.at[s],
                       at3(lax.rem(me3 + r, n3))).start()

    send_boundary(back_ref, ret_ref, 1, *BATCHES[3])

    def final(s, rows, count):
        first, width = strips[s][:2]
        return gw_ref.at[core, pl.ds(rows, count), pl.ds(first, width)]

    for s, (first, width, (n1, me1, _), (n2, me2, at2), (n3, _, _)) in enumerate(strips):
        with jax.named_scope("gather_one_%d" % s):
            wait(three_ref[s].at[pl.ds(0, 16 * (n3 - 1))], three_recv.at[s])
            done = three_ref[s][0:16, :].astype(F32)
            for i in range(1, n3):
                done = done + three_ref[s][16 * i:16 * i + 16, :].astype(F32)
            row = pl.multiple_of(me1 * (512 // n1) + me2 * 16, 16)
            gw_ref[core, pl.ds(row, 16), pl.ds(first, width)] = done.astype(BF16)
            for r in range(1, n2):
                remote(final(s, row, 16), final(s, row, 16), ag1_recv.at[s],
                       at2(lax.rem(me2 + r, n2))).start()

    send_boundary(back_ref, ret_ref, 1, *BATCHES[4])

    def forward(s, row, count):
        remote(final(s, row, count), final(s, row, count), fin_recv, sibling).start()

    units = []
    for s, (_, _, (n1, _, _), _, _) in enumerate(strips):
        units.append(units[-1] + (4 if strips[s - 1][2][0] == 4 else 1) if s else 0)

    for s in sorted(range(len(strips)), key=lambda s: strips[s][2][0] == 4):
        _, _, (n1, me1, at1), (n2, _, _), _ = strips[s]
        with jax.named_scope("gather_two_%d" % s):
            rows1 = 512 // n1
            wait(final(s, 0, 16 * (n2 - 1)), ag1_recv.at[s])
            row = pl.multiple_of(me1 * rows1, rows1)
            for r in range(1, n1):
                unit = units[s] + me1 if n1 == 4 else units[s]
                remote(final(s, row, rows1), final(s, row, rows1), ag2_recv.at[unit],
                       at1(lax.rem(me1 + r, n1))).start()
            if n1 == 4:
                forward(s, row, rows1)

    send_boundary(back_ref, ret_ref, 1, *BATCHES[5])

    with jax.named_scope("forward"):
        for s, (_, _, (n1, me1, _), _, _) in enumerate(strips):
            if n1 == 4:
                for r in range(1, 4):
                    i = lax.rem(me1 + r, 4)
                    row = pl.multiple_of(i * 128, 128)
                    wait(final(s, row, 128), ag2_recv.at[units[s] + i])
                    forward(s, row, 128)
            else:
                wait(final(s, 0, 448), ag2_recv.at[units[s]])
                forward(s, 0, 512)

    with jax.named_scope("wait_grads"):
        wait_boundary(ret_ref, 1)
    with jax.named_scope("feature_grads"):
        returned = dot(sel_ref[...], ret_ref[...])
        gfeat_ref[...] = (
            base_ref[...] + jnp.concatenate([returned[0:128], returned[128:256]], axis=1)
        ).astype(BF16)

    with jax.named_scope("finish"):
        wait(all_sent_ref, sent)
        wait(gw_ref.at[other], fin_recv)


def write_kernel(gfeat_in, gw_in, gfeat_ref, gws_ref, gwn_ref, wide_ref, sem):
    copies = [pltpu.make_async_copy(gfeat_in, gfeat_ref, sem.at[0])]
    copies[0].start()
    for c, ref in enumerate((gws_ref, gwn_ref)):
        for piece in range(4):
            rows = pl.ds(128 * piece, 128)
            wide_ref[c, rows, :] = gw_in[c, rows, :].astype(F32)
            copy = pltpu.make_async_copy(
                wide_ref.at[c, rows], ref.at[rows], sem.at[1 + 4 * c + piece])
            copy.start()
            copies.append(copy)
    for copy in copies:
        copy.wait()


def strip_scratch(shape, dtype):
    return tuple(
        pltpu.VMEM(shape(width, 4 if order[0] == "x" else 8), dtype) for _, width, order in STRIPS
    )


def sent_rows():
    length = {"x": 4, "y": 8, "z": 8}
    rows = 2 * 63 * 8 + 2 * 128 + 512
    for _, width, order in STRIPS:
        n1, n2, n3 = (length[axis] for axis in order)
        steps = 2 * (512 - 512 // n1) + 2 * 16 * (n2 - 1) + 16 * (n3 - 1)
        rows += steps * width // 512
    return rows


def local(features, w_self, w_neigh, cotangent, neighbors, send_rows, send_count):
    vmem = pl.BlockSpec(memory_space=pltpu.VMEM)
    hbm = pl.BlockSpec(memory_space=pltpu.HBM)
    dma = pltpu.SemaphoreType.DMA
    grad_features, grads = pl.pallas_call(
        kernel,
        out_shape=(
            pltpu.VMEM((128, 512), BF16),
            pltpu.VMEM((2, 512, 512), BF16),
        ),
        in_specs=[hbm] * 7,
        out_specs=(vmem, vmem),
        scratch_shapes=[
            pltpu.VMEM((128, 512), BF16),
            pltpu.VMEM((2, 512, 512), BF16),
            pltpu.VMEM((128, 512), BF16),
            pltpu.VMEM((16, 128), jnp.int32),
            pltpu.VMEM((8, 64), jnp.int32),
            pltpu.VMEM((1, 64), jnp.int32),
            pltpu.VMEM((256, 1024), BF16),
            pltpu.VMEM((256, 1024), BF16),
            pltpu.VMEM((1024, 256), BF16),
            pltpu.VMEM((1024, 256), BF16),
            pltpu.VMEM((1024, 256), BF16),
            pltpu.VMEM((1024, 256), BF16),
            pltpu.VMEM((1024, 256), BF16),
            pltpu.VMEM((2, 512, 128), BF16),
            pltpu.VMEM((512, 128), BF16),
            pltpu.VMEM((256, 512), BF16),
            pltpu.VMEM((512, 512), F32),
            strip_scratch(lambda w, n: (512, w), BF16),
            strip_scratch(lambda w, n: (512, w), BF16),
            strip_scratch(lambda w, n: (512 // n, w), F32),
            strip_scratch(lambda w, n: (512 // n, w), BF16),
            strip_scratch(lambda w, n: (512 // n, w), BF16),
            strip_scratch(lambda w, n: (128, w), BF16),
            pltpu.VMEM((128, 512), F32),
            pltpu.VMEM((sent_rows(), 512), BF16),
            dma((6,)), dma, dma((2,)), dma((2,)), *([dma((len(STRIPS),))] * 4),
            dma((sum(4 if order[0] == "x" else 1 for _, _, order in STRIPS),)), dma,
        ],
        compiler_params=pltpu.CompilerParams(
            collective_id=0, has_side_effects=True, vmem_limit_bytes=40 << 20
        ),
        name="sage_backward",
    )(*(
        pltpu.with_memory_space_constraint(array, pltpu.HBM)
        for array in (
            features, w_self, w_neigh, cotangent, neighbors.T,
            send_rows.reshape(64, 8).T, send_count.reshape(1, 64),
        )
    ))
    return pl.pallas_call(
        write_kernel,
        out_shape=(
            jax.ShapeDtypeStruct((128, 512), BF16),
            jax.ShapeDtypeStruct((512, 512), F32),
            jax.ShapeDtypeStruct((512, 512), F32),
        ),
        in_specs=[vmem, vmem],
        out_specs=(hbm, hbm, hbm),
        scratch_shapes=[pltpu.VMEM((2, 512, 512), F32), dma((9,))],
        compiler_params=pltpu.CompilerParams(vmem_limit_bytes=8 << 20),
        name="write_results",
    )(grad_features, grads)


def solution(mesh):
    placed = (
        P(("grp", "dom"), None),
        P(),
        P(),
        P(("grp", "dom"), None),
        P(("grp", "dom"), None),
        P("grp", "dom", None, None),
        P("grp", "dom", None),
    )
    return jax.shard_map(
        local,
        mesh=mesh,
        in_specs=placed,
        out_specs=(P(("grp", "dom"), None), P(), P()),
        check_vma=False,
    )
```

```python
import functools

import jax
import jax.numpy as jnp
from jax import lax
from jax.experimental import pallas as pl
from jax.experimental.pallas import tpu as pltpu
from jax.sharding import PartitionSpec as P

MESH = pl.DeviceIdType.MESH
F32 = jnp.float32
BF16 = jnp.bfloat16


STRIPS = ((0, 256, "xzy"), (256, 128, "zxy"), (384, 128, "yxz"))
BATCHES = ((), ((0, 31),), (), (), ((31, 63),), ())


def dot(left, right, left_dim=1, right_dim=0):
    return lax.dot_general(
        left, right, (((left_dim,), (right_dim,)), ((), ())), preferred_element_type=F32
    )


def iota(shape, dim):
    return lax.broadcasted_iota(jnp.int32, shape, dim)


def gelu_slope(v):
    root = 0.7978845608028654
    square = v * v
    t = jnp.tanh(root * (v + 0.044715 * square * v))
    return 0.5 * (1.0 + t) + (0.5 * root) * v * (1.0 - t * t) * (1.0 + 0.134145 * square)


def kernel(
    feat_hbm, ws_hbm, wn_hbm, cot_hbm, nb_hbm, rows_hbm, count_hbm,
    gfeat_ref, gw_ref,
    feat_ref, w_ref, cot_ref, nb_ref, rows_ref, count_ref,
    sel_ref, adj_ref, adjt_ref, out_ref, halo_ref, back_ref, ret_ref,
    lt_ref, lt_pair, gp_ref, own_ref, one_out, one_in, sum_ref, two_out, two_in, three_ref, base_ref,
    all_sent_ref, load_sem, sent, a2a_recv, pair_recv, one_recv, two_recv, three_recv, ag1_recv,
    ag2_recv, fin_recv,
):
    grp = lax.axis_index("grp")
    dom = lax.axis_index("dom")
    core = lax.rem(dom, 2)
    other = 1 - core
    sibling = {"dom": dom + 1 - 2 * core}
    y = lax.rem(dom // 2, 8)
    x = dom // 16

    axis_x = (4, x, lambda i: {"dom": i * 16 + y * 2 + core})
    axis_y = (8, y, lambda i: {"dom": x * 16 + i * 2 + core})
    axis_z = (8, grp, lambda i: {"grp": i})
    axes = {"x": axis_x, "y": axis_y, "z": axis_z}
    strips = tuple(
        (first, width) + tuple(axes[name] for name in order) for first, width, order in STRIPS
    )

    def dom_peer(r):
        return lax.rem(dom + r, 64)

    far_first = (4, 3, 5, 2, 6, 1, 7, 0)

    def far_peer(o, dy):
        return (
            lax.rem(x + o // 2, 4) * 16 + lax.rem(y + dy, 8) * 2 + lax.rem(core + lax.rem(o, 2), 2))

    def loop(first, last, body):
        lax.fori_loop(first, last, lambda i, c: (body(i), c)[1], 0)

    def remote(src, dst, recv, device):
        return pltpu.make_async_remote_copy(
            src_ref=src, dst_ref=dst, send_sem=sent, recv_sem=recv,
            device_id=device, device_id_type=MESH,
        )

    def wait(ref, sem):
        pltpu.make_async_copy(ref, ref, sem).wait()

    def part(i, size):
        return pl.ds(pl.multiple_of(i * size, size), size)

    loads = [
        pltpu.make_async_copy(src, dst, load_sem.at[i])
        for i, src, dst in [
            (0, rows_hbm, rows_ref), (1, count_hbm, count_ref), (2, feat_hbm, feat_ref),
            (3, nb_hbm, nb_ref), (4, cot_hbm, cot_ref),
            (5, ws_hbm, w_ref.at[0]), (5, wn_hbm, w_ref.at[1]),
        ]
    ]
    for load in loads:
        load.start()

    barrier = pltpu.get_barrier_semaphore()
    with jax.named_scope("greet"):
        loop(1, 64, lambda r: pl.semaphore_signal(
            barrier, inc=1, device_id={"dom": dom_peer(r)}, device_id_type=MESH))
        loop(1, 8, lambda r: pl.semaphore_signal(
            barrier, inc=1, device_id={"grp": lax.rem(grp + r, 8)}, device_id_type=MESH))

    with jax.named_scope("outgoing"):
        col = iota((1, 1024), 1)
        slot_of = jnp.bitwise_and(col, 7)
        half_of = jnp.bitwise_and(lax.shift_right_logical(col, 3), 1)
        in_peer = (iota((64, 1024), 0) == lax.shift_right_logical(col, 4)).astype(BF16)
        for load in loads[:3]:
            load.wait()
        counts = jnp.broadcast_to(count_ref[...], (8, 64))
        table = jnp.concatenate([rows_ref[...], counts], axis=0).astype(F32).astype(BF16)
        spread = dot(table, in_peer)
        row = jnp.sum(
            jnp.where(iota((8, 1024), 0) == slot_of, spread[0:8], 0.0), axis=0, keepdims=True)
        live = spread[8:9] > slot_of.astype(F32)
        target = jnp.where(live, row + 128.0 * half_of.astype(F32), 512.0)
        sel_ref[...] = (iota((256, 1024), 0).astype(F32) == target).astype(BF16)
        feat = feat_ref[...]
        feat2 = jnp.concatenate([feat[:, :256], feat[:, 256:]], axis=0)
        out_ref[...] = dot(sel_ref[...], feat2, 0, 0).astype(BF16)

    with jax.named_scope("barrier"):
        pl.semaphore_wait(barrier, 70)

    def send_block(src, dst, k, peer):
        remote(src.at[part(peer, 16)], dst.at[part(dom, 16)], a2a_recv.at[k], {"dom": peer}).start()

    def send_far_first(src, dst, k):
        def one(i):
            for dy in far_first:
                send_block(src, dst, k, far_peer(7 - i, dy))
        loop(0, 7, one)
        for dy in far_first[:7]:
            send_block(src, dst, k, far_peer(0, dy))

    def send_boundary(src, dst, k, *distances):
        for first, last in distances:
            loop(first, last, lambda r: send_block(src, dst, k, dom_peer(r + 1)))

    def keep_boundary(src, dst):
        dst[part(dom, 16), :] = src[part(dom, 16), :]

    def wait_boundary(dst, k):
        wait(dst.at[pl.ds(0, 63 * 16)], a2a_recv.at[k])

    with jax.named_scope("send_rows"):
        send_far_first(out_ref, halo_ref, 0)
        keep_boundary(out_ref, halo_ref)

    with jax.named_scope("adjacency"):
        loads[3].wait()
        nb = nb_ref[...]
        entry = nb - 128
        place_of = (
            lax.shift_left(lax.shift_right_arithmetic(entry, 3), 4) + jnp.bitwise_and(entry, 7))
        row_ids = iota((1024, 128), 0)
        count = jnp.zeros((1024, 128), F32)
        for k in range(8, 16):
            count = count + jnp.where(row_ids == place_of[k:k + 1, :], 1.0, 0.0)
        lower = count.T
        adjt_ref[:, 0:128] = count.astype(BF16)
        adjt_ref[:, 128:256] = pltpu.roll(count, 8, 0).astype(BF16)
        adj_ref[0:128, :] = lower.astype(BF16)
        adj_ref[128:256, :] = pltpu.roll(lower, 8, 1).astype(BF16)
        own_ids = iota((128, 128), 0)
        own_t = jnp.zeros((128, 128), F32)
        for k in range(8):
            own_t = own_t + jnp.where(own_ids == nb[k:k + 1, :], 1.0, 0.0)
        own_adj = own_t.T.astype(BF16)
        own_adj_t = own_t.astype(BF16)
        own_sum = dot(own_adj, feat)
        lt_ref[0] = feat.astype(F32).T.astype(BF16)
        loads[4].wait()
        wait(w_ref, load_sem.at[5])
        pre_self = dot(feat, w_ref[0])

    with jax.named_scope("wait_rows"):
        wait_boundary(halo_ref, 0)
    with jax.named_scope("grad_pre"):
        halo_sum = dot(adj_ref[...], halo_ref[...])
        summed = own_sum + jnp.concatenate([halo_sum[0:128], halo_sum[128:256]], axis=1)
        agg = (summed * (1.0 / 16.0)).astype(BF16)
        lt_ref[1] = agg.astype(F32).T.astype(BF16)
        remote(lt_ref.at[other], lt_pair, pair_recv.at[0], sibling).start()
        pre = pre_self + dot(agg, w_ref[1])
        grad_pre = (cot_ref[...].astype(F32) * gelu_slope(pre)).astype(BF16)
        gp_ref[0:128, :] = grad_pre
        remote(gp_ref.at[pl.ds(0, 128)], gp_ref.at[pl.ds(128, 128)], pair_recv.at[1],
               sibling).start()

    with jax.named_scope("boundary_grads"):
        grad_agg = (dot(grad_pre, w_ref[1], 1, 1) * (1.0 / 16.0)).astype(BF16)
        grad_agg2 = jnp.concatenate([grad_agg[:, :256], grad_agg[:, 256:]], axis=0)
        back_ref[...] = dot(adjt_ref[...], grad_agg2).astype(BF16)

    def send_one(s, i):
        first, width, (n, me, at), _, _ = strips[s]
        rows = part(i, 512 // n)
        one_out[s][rows, :] = own_ref[rows, pl.ds(first, width)].astype(BF16)

        @pl.when(i != me)
        def _():
            remote(one_out[s].at[rows], one_in[s].at[part(me, 512 // n)], one_recv.at[s],
                   at(i)).start()

    with jax.named_scope("step_one"):
        wait(lt_pair, pair_recv.at[0])
        wait(gp_ref.at[pl.ds(0, 128)], pair_recv.at[1])
        both = gp_ref[...]
        scale = 65536.0 ** -0.5
        for r in range(4):
            i = lax.rem(x + 1 + r, 4)
            rows = part(i, 128)
            left = jnp.concatenate([lt_ref[core, rows, :], lt_pair[rows, :]], axis=1)
            own_ref[rows, :] = dot(left, both) * scale
            for s, (_, _, (n1, _, _), _, _) in enumerate(strips):
                if n1 == 8 or r < 3:
                    for j in range(n1 // 4):
                        send_one(s, n1 // 4 * i + j)

    with jax.named_scope("send_grads"):
        send_boundary(back_ref, ret_ref, 1, *BATCHES[0])
        keep_boundary(back_ref, ret_ref)
    with jax.named_scope("base"):
        base_ref[...] = dot(grad_pre, w_ref[0], 1, 1) + dot(own_adj_t, grad_agg)

    for s, (first, width, (n1, me1, _), (n2, me2, at2), _) in enumerate(strips):
        with jax.named_scope("step_two_%d" % s):
            rows1 = 512 // n1
            mine = part(me1, rows1)
            cols = pl.ds(first, width)
            total = own_ref[mine, cols]
            wait(one_in[s].at[pl.ds(0, 512 - rows1)], one_recv.at[s])
            for r in range(1, n1):
                total = total + one_in[s][part(lax.rem(me1 + r, n1), rows1), :].astype(F32)
            sum_ref[s][...] = total
            two_out[s][...] = total.astype(BF16)
            for r in range(1, n2):
                i = lax.rem(me2 + r, n2)
                remote(two_out[s].at[part(i, 16)], two_in[s].at[part(me2, 16)],
                       two_recv.at[s], at2(i)).start()
            if s == 0:
                send_boundary(back_ref, ret_ref, 1, *BATCHES[1])

    send_boundary(back_ref, ret_ref, 1, *BATCHES[2])

    for s, (_, _, _, (n2, me2, _), (n3, me3, at3)) in enumerate(strips):
        with jax.named_scope("step_three_%d" % s):
            small = sum_ref[s][part(me2, 16), :]
            wait(two_in[s].at[pl.ds(0, 16 * (n2 - 1))], two_recv.at[s])
            for r in range(1, n2):
                small = small + two_in[s][part(lax.rem(me2 + r, n2), 16), :].astype(F32)
            three_ref[s][part(me3, 16), :] = small.astype(BF16)
            for r in range(1, n3):
                here = three_ref[s].at[part(me3, 16)]
                remote(here, here, three_recv.at[s],
                       at3(lax.rem(me3 + r, n3))).start()

    send_boundary(back_ref, ret_ref, 1, *BATCHES[3])

    def final(s, rows, count):
        first, width = strips[s][:2]
        return gw_ref.at[core, pl.ds(rows, count), pl.ds(first, width)]

    for s, (first, width, (n1, me1, _), (n2, me2, at2), (n3, _, _)) in enumerate(strips):
        with jax.named_scope("gather_one_%d" % s):
            wait(three_ref[s].at[pl.ds(0, 16 * (n3 - 1))], three_recv.at[s])
            done = three_ref[s][0:16, :].astype(F32)
            for i in range(1, n3):
                done = done + three_ref[s][16 * i:16 * i + 16, :].astype(F32)
            row = pl.multiple_of(me1 * (512 // n1) + me2 * 16, 16)
            gw_ref[core, pl.ds(row, 16), pl.ds(first, width)] = done.astype(BF16)
            for r in range(1, n2):
                remote(final(s, row, 16), final(s, row, 16), ag1_recv.at[s],
                       at2(lax.rem(me2 + r, n2))).start()

    send_boundary(back_ref, ret_ref, 1, *BATCHES[4])

    def forward(s, row, count):
        remote(final(s, row, count), final(s, row, count), fin_recv, sibling).start()

    units = []
    for s, (_, _, (n1, _, _), _, _) in enumerate(strips):
        units.append(units[-1] + (4 if strips[s - 1][2][0] == 4 else 1) if s else 0)

    for s, (_, _, (n1, me1, at1), (n2, _, _), _) in enumerate(strips):
        with jax.named_scope("gather_two_%d" % s):
            rows1 = 512 // n1
            wait(final(s, 0, 16 * (n2 - 1)), ag1_recv.at[s])
            row = pl.multiple_of(me1 * rows1, rows1)
            for r in range(1, n1):
                unit = units[s] + me1 if n1 == 4 else units[s]
                remote(final(s, row, rows1), final(s, row, rows1), ag2_recv.at[unit],
                       at1(lax.rem(me1 + r, n1))).start()
            if n1 == 4:
                forward(s, row, rows1)

    send_boundary(back_ref, ret_ref, 1, *BATCHES[5])

    with jax.named_scope("forward"):
        for s, (_, _, (n1, me1, _), _, _) in enumerate(strips):
            if n1 == 4:
                for r in range(1, 4):
                    i = lax.rem(me1 + r, 4)
                    row = pl.multiple_of(i * 128, 128)
                    wait(final(s, row, 128), ag2_recv.at[units[s] + i])
                    forward(s, row, 128)
            else:
                wait(final(s, 0, 448), ag2_recv.at[units[s]])
                forward(s, 0, 512)

    with jax.named_scope("wait_grads"):
        wait_boundary(ret_ref, 1)
    with jax.named_scope("feature_grads"):
        returned = dot(sel_ref[...], ret_ref[...])
        gfeat_ref[...] = (
            base_ref[...] + jnp.concatenate([returned[0:128], returned[128:256]], axis=1)
        ).astype(BF16)

    with jax.named_scope("finish"):
        wait(all_sent_ref, sent)
        wait(gw_ref.at[other], fin_recv)


def write_kernel(gfeat_in, gw_in, gfeat_ref, gws_ref, gwn_ref, wide_ref, sem):
    copies = [pltpu.make_async_copy(gfeat_in, gfeat_ref, sem.at[0])]
    copies[0].start()
    for c, ref in enumerate((gws_ref, gwn_ref)):
        for piece in range(4):
            rows = pl.ds(128 * piece, 128)
            wide_ref[c, rows, :] = gw_in[c, rows, :].astype(F32)
            copy = pltpu.make_async_copy(
                wide_ref.at[c, rows], ref.at[rows], sem.at[1 + 4 * c + piece])
            copy.start()
            copies.append(copy)
    for copy in copies:
        copy.wait()


def strip_scratch(shape, dtype):
    return tuple(
        pltpu.VMEM(shape(width, 4 if order[0] == "x" else 8), dtype) for _, width, order in STRIPS
    )


def sent_rows():
    length = {"x": 4, "y": 8, "z": 8}
    rows = 2 * 63 * 8 + 2 * 128 + 512
    for _, width, order in STRIPS:
        n1, n2, n3 = (length[axis] for axis in order)
        steps = 2 * (512 - 512 // n1) + 2 * 16 * (n2 - 1) + 16 * (n3 - 1)
        rows += steps * width // 512
    return rows


def local(features, w_self, w_neigh, cotangent, neighbors, send_rows, send_count):
    vmem = pl.BlockSpec(memory_space=pltpu.VMEM)
    hbm = pl.BlockSpec(memory_space=pltpu.HBM)
    dma = pltpu.SemaphoreType.DMA
    grad_features, grads = pl.pallas_call(
        kernel,
        out_shape=(
            pltpu.VMEM((128, 512), BF16),
            pltpu.VMEM((2, 512, 512), BF16),
        ),
        in_specs=[hbm] * 7,
        out_specs=(vmem, vmem),
        scratch_shapes=[
            pltpu.VMEM((128, 512), BF16),
            pltpu.VMEM((2, 512, 512), BF16),
            pltpu.VMEM((128, 512), BF16),
            pltpu.VMEM((16, 128), jnp.int32),
            pltpu.VMEM((8, 64), jnp.int32),
            pltpu.VMEM((1, 64), jnp.int32),
            pltpu.VMEM((256, 1024), BF16),
            pltpu.VMEM((256, 1024), BF16),
            pltpu.VMEM((1024, 256), BF16),
            pltpu.VMEM((1024, 256), BF16),
            pltpu.VMEM((1024, 256), BF16),
            pltpu.VMEM((1024, 256), BF16),
            pltpu.VMEM((1024, 256), BF16),
            pltpu.VMEM((2, 512, 128), BF16),
            pltpu.VMEM((512, 128), BF16),
            pltpu.VMEM((256, 512), BF16),
            pltpu.VMEM((512, 512), F32),
            strip_scratch(lambda w, n: (512, w), BF16),
            strip_scratch(lambda w, n: (512, w), BF16),
            strip_scratch(lambda w, n: (512 // n, w), F32),
            strip_scratch(lambda w, n: (512 // n, w), BF16),
            strip_scratch(lambda w, n: (512 // n, w), BF16),
            strip_scratch(lambda w, n: (128, w), BF16),
            pltpu.VMEM((128, 512), F32),
            pltpu.VMEM((sent_rows(), 512), BF16),
            dma((6,)), dma, dma((2,)), dma((2,)), *([dma((len(STRIPS),))] * 4),
            dma((sum(4 if order[0] == "x" else 1 for _, _, order in STRIPS),)), dma,
        ],
        compiler_params=pltpu.CompilerParams(
            collective_id=0, has_side_effects=True, vmem_limit_bytes=40 << 20
        ),
        name="sage_backward",
    )(*(
        pltpu.with_memory_space_constraint(array, pltpu.HBM)
        for array in (
            features, w_self, w_neigh, cotangent, neighbors.T,
            send_rows.reshape(64, 8).T, send_count.reshape(1, 64),
        )
    ))
    return pl.pallas_call(
        write_kernel,
        out_shape=(
            jax.ShapeDtypeStruct((128, 512), BF16),
            jax.ShapeDtypeStruct((512, 512), F32),
            jax.ShapeDtypeStruct((512, 512), F32),
        ),
        in_specs=[vmem, vmem],
        out_specs=(hbm, hbm, hbm),
        scratch_shapes=[pltpu.VMEM((2, 512, 512), F32), dma((9,))],
        compiler_params=pltpu.CompilerParams(vmem_limit_bytes=8 << 20),
        name="write_results",
    )(grad_features, grads)


def solution(mesh):
    placed = (
        P(("grp", "dom"), None),
        P(),
        P(),
        P(("grp", "dom"), None),
        P(("grp", "dom"), None),
        P("grp", "dom", None, None),
        P("grp", "dom", None),
    )
    return jax.shard_map(
        local,
        mesh=mesh,
        in_specs=placed,
        out_specs=(P(("grp", "dom"), None), P(), P()),
        check_vma=False,
    )
```

```python
import functools

import jax
import jax.numpy as jnp
from jax import lax
from jax.experimental import pallas as pl
from jax.experimental.pallas import tpu as pltpu
from jax.sharding import PartitionSpec as P

MESH = pl.DeviceIdType.MESH
F32 = jnp.float32
BF16 = jnp.bfloat16


STRIPS = ((0, 256, "xzy"), (256, 128, "zxy"), (384, 128, "yxz"))
BATCHES = ((), ((0, 31),), (), (), ((31, 63),), ())


def dot(left, right, left_dim=1, right_dim=0):
    return lax.dot_general(
        left, right, (((left_dim,), (right_dim,)), ((), ())), preferred_element_type=F32
    )


def iota(shape, dim):
    return lax.broadcasted_iota(jnp.int32, shape, dim)


def gelu_slope(v):
    root = 0.7978845608028654
    square = v * v
    t = jnp.tanh(root * (v + 0.044715 * square * v))
    return 0.5 * (1.0 + t) + (0.5 * root) * v * (1.0 - t * t) * (1.0 + 0.134145 * square)


def kernel(
    feat_hbm, ws_hbm, wn_hbm, cot_hbm, nb_hbm, rows_hbm, count_hbm,
    gfeat_ref, gw_ref,
    feat_ref, w_ref, cot_ref, nb_ref, rows_ref, count_ref,
    sel_ref, adj_ref, adjt_ref, out_ref, halo_ref, back_ref, ret_ref,
    lt_ref, lt_pair, gp_ref, own_ref, one_out, one_in, sum_ref, two_out, two_in, three_ref, base_ref,
    all_sent_ref, load_sem, sent, a2a_recv, pair_recv, one_recv, two_recv, three_recv, ag1_recv,
    ag2_recv, fin_recv,
):
    grp = lax.axis_index("grp")
    dom = lax.axis_index("dom")
    core = lax.rem(dom, 2)
    other = 1 - core
    sibling = {"dom": dom + 1 - 2 * core}
    y = lax.rem(dom // 2, 8)
    x = dom // 16

    axis_x = (4, x, lambda i: {"dom": i * 16 + y * 2 + core})
    axis_y = (8, y, lambda i: {"dom": x * 16 + i * 2 + core})
    axis_z = (8, grp, lambda i: {"grp": i})
    axes = {"x": axis_x, "y": axis_y, "z": axis_z}
    strips = tuple(
        (first, width) + tuple(axes[name] for name in order) for first, width, order in STRIPS
    )

    def dom_peer(r):
        return lax.rem(dom + r, 64)

    far_first = (4, 3, 5, 2, 6, 1, 7, 0)

    def far_peer(o, dy):
        return (
            lax.rem(x + o // 2, 4) * 16 + lax.rem(y + dy, 8) * 2 + lax.rem(core + lax.rem(o, 2), 2))

    def loop(first, last, body):
        lax.fori_loop(first, last, lambda i, c: (body(i), c)[1], 0)

    def remote(src, dst, recv, device):
        return pltpu.make_async_remote_copy(
            src_ref=src, dst_ref=dst, send_sem=sent, recv_sem=recv,
            device_id=device, device_id_type=MESH,
        )

    def wait(ref, sem):
        pltpu.make_async_copy(ref, ref, sem).wait()

    def part(i, size):
        return pl.ds(pl.multiple_of(i * size, size), size)

    loads = [
        pltpu.make_async_copy(src, dst, load_sem.at[i])
        for i, src, dst in [
            (0, rows_hbm, rows_ref), (1, count_hbm, count_ref), (2, feat_hbm, feat_ref),
            (3, nb_hbm, nb_ref), (4, cot_hbm, cot_ref),
            (5, ws_hbm, w_ref.at[0]), (5, wn_hbm, w_ref.at[1]),
        ]
    ]
    for load in loads:
        load.start()

    barrier = pltpu.get_barrier_semaphore()
    with jax.named_scope("greet"):
        loop(1, 64, lambda r: pl.semaphore_signal(
            barrier, inc=1, device_id={"dom": dom_peer(r)}, device_id_type=MESH))
        loop(1, 8, lambda r: pl.semaphore_signal(
            barrier, inc=1, device_id={"grp": lax.rem(grp + r, 8)}, device_id_type=MESH))

    with jax.named_scope("outgoing"):
        col = iota((1, 1024), 1)
        slot_of = jnp.bitwise_and(col, 7)
        half_of = jnp.bitwise_and(lax.shift_right_logical(col, 3), 1)
        in_peer = (iota((64, 1024), 0) == lax.shift_right_logical(col, 4)).astype(BF16)
        for load in loads[:3]:
            load.wait()
        counts = jnp.broadcast_to(count_ref[...], (8, 64))
        table = jnp.concatenate([rows_ref[...], counts], axis=0).astype(F32).astype(BF16)
        spread = dot(table, in_peer)
        row = jnp.sum(
            jnp.where(iota((8, 1024), 0) == slot_of, spread[0:8], 0.0), axis=0, keepdims=True)
        live = spread[8:9] > slot_of.astype(F32)
        target = jnp.where(live, row + 128.0 * half_of.astype(F32), 512.0)
        sel_ref[...] = (iota((256, 1024), 0).astype(F32) == target).astype(BF16)
        feat = feat_ref[...]
        feat2 = jnp.concatenate([feat[:, :256], feat[:, 256:]], axis=0)
        out_ref[...] = dot(sel_ref[...], feat2, 0, 0).astype(BF16)

    with jax.named_scope("barrier"):
        pl.semaphore_wait(barrier, 70)

    def send_block(src, dst, k, peer):
        remote(src.at[part(peer, 16)], dst.at[part(dom, 16)], a2a_recv.at[k], {"dom": peer}).start()

    def send_far_first(src, dst, k):
        def one(i):
            for dy in far_first:
                send_block(src, dst, k, far_peer(7 - i, dy))
        loop(0, 7, one)
        for dy in far_first[:7]:
            send_block(src, dst, k, far_peer(0, dy))

    def send_boundary(src, dst, k, *distances):
        for first, last in distances:
            loop(first, last, lambda r: send_block(src, dst, k, dom_peer(r + 1)))

    def keep_boundary(src, dst):
        dst[part(dom, 16), :] = src[part(dom, 16), :]

    def wait_boundary(dst, k):
        wait(dst.at[pl.ds(0, 63 * 16)], a2a_recv.at[k])

    with jax.named_scope("send_rows"):
        send_far_first(out_ref, halo_ref, 0)
        keep_boundary(out_ref, halo_ref)

    with jax.named_scope("adjacency"):
        loads[3].wait()
        nb = nb_ref[...]
        entry = nb - 128
        place_of = (
            lax.shift_left(lax.shift_right_arithmetic(entry, 3), 4) + jnp.bitwise_and(entry, 7))
        row_ids = iota((1024, 128), 0)
        count = jnp.zeros((1024, 128), F32)
        for k in range(8, 16):
            count = count + jnp.where(row_ids == place_of[k:k + 1, :], 1.0, 0.0)
        lower = count.T
        adjt_ref[:, 0:128] = count.astype(BF16)
        adjt_ref[:, 128:256] = pltpu.roll(count, 8, 0).astype(BF16)
        adj_ref[0:128, :] = lower.astype(BF16)
        adj_ref[128:256, :] = pltpu.roll(lower, 8, 1).astype(BF16)
        own_ids = iota((128, 128), 0)
        own_t = jnp.zeros((128, 128), F32)
        for k in range(8):
            own_t = own_t + jnp.where(own_ids == nb[k:k + 1, :], 1.0, 0.0)
        own_adj = own_t.T.astype(BF16)
        own_adj_t = own_t.astype(BF16)
        own_sum = dot(own_adj, feat)
        lt_ref[0] = feat.astype(F32).T.astype(BF16)
        loads[4].wait()
        wait(w_ref, load_sem.at[5])
        pre_self = dot(feat, w_ref[0])

    with jax.named_scope("wait_rows"):
        wait_boundary(halo_ref, 0)
    with jax.named_scope("grad_pre"):
        halo_sum = dot(adj_ref[...], halo_ref[...])
        summed = own_sum + jnp.concatenate([halo_sum[0:128], halo_sum[128:256]], axis=1)
        agg = (summed * (1.0 / 16.0)).astype(BF16)
        lt_ref[1] = agg.astype(F32).T.astype(BF16)
        remote(lt_ref.at[other], lt_pair, pair_recv.at[0], sibling).start()
        pre = pre_self + dot(agg, w_ref[1])
        grad_pre = (cot_ref[...].astype(F32) * gelu_slope(pre)).astype(BF16)
        gp_ref[0:128, :] = grad_pre
        remote(gp_ref.at[pl.ds(0, 128)], gp_ref.at[pl.ds(128, 128)], pair_recv.at[1],
               sibling).start()

    with jax.named_scope("boundary_grads"):
        grad_agg = (dot(grad_pre, w_ref[1], 1, 1) * (1.0 / 16.0)).astype(BF16)
        grad_agg2 = jnp.concatenate([grad_agg[:, :256], grad_agg[:, 256:]], axis=0)
        back_ref[...] = dot(adjt_ref[...], grad_agg2).astype(BF16)

    def send_one(s, i):
        first, width, (n, me, at), _, _ = strips[s]
        rows = part(i, 512 // n)
        one_out[s][rows, :] = own_ref[rows, pl.ds(first, width)].astype(BF16)

        @pl.when(i != me)
        def _():
            remote(one_out[s].at[rows], one_in[s].at[part(me, 512 // n)], one_recv.at[s],
                   at(i)).start()

    with jax.named_scope("step_one"):
        wait(lt_pair, pair_recv.at[0])
        wait(gp_ref.at[pl.ds(0, 128)], pair_recv.at[1])
        both = gp_ref[...]
        scale = 65536.0 ** -0.5
        for r in range(4):
            i = lax.rem(x + 1 + r, 4)
            rows = part(i, 128)
            left = jnp.concatenate([lt_ref[core, rows, :], lt_pair[rows, :]], axis=1)
            own_ref[rows, :] = dot(left, both) * scale
            for s, (_, _, (n1, _, _), _, _) in enumerate(strips):
                if n1 == 8 or r < 3:
                    for j in range(n1 // 4):
                        send_one(s, n1 // 4 * i + j)

    with jax.named_scope("send_grads"):
        send_boundary(back_ref, ret_ref, 1, *BATCHES[0])
        keep_boundary(back_ref, ret_ref)
    with jax.named_scope("base"):
        base_ref[...] = dot(grad_pre, w_ref[0], 1, 1) + dot(own_adj_t, grad_agg)

    for s, (first, width, (n1, me1, _), (n2, me2, at2), _) in enumerate(strips):
        with jax.named_scope("step_two_%d" % s):
            rows1 = 512 // n1
            mine = part(me1, rows1)
            cols = pl.ds(first, width)
            total = own_ref[mine, cols]
            wait(one_in[s].at[pl.ds(0, 512 - rows1)], one_recv.at[s])
            for r in range(1, n1):
                total = total + one_in[s][part(lax.rem(me1 + r, n1), rows1), :].astype(F32)
            sum_ref[s][...] = total
            two_out[s][...] = total.astype(BF16)
            for r in range(1, n2):
                i = lax.rem(me2 + r, n2)
                remote(two_out[s].at[part(i, 16)], two_in[s].at[part(me2, 16)],
                       two_recv.at[s], at2(i)).start()
            if s == 0:
                send_boundary(back_ref, ret_ref, 1, *BATCHES[1])

    send_boundary(back_ref, ret_ref, 1, *BATCHES[2])

    for s, (_, _, _, (n2, me2, _), (n3, me3, at3)) in enumerate(strips):
        with jax.named_scope("step_three_%d" % s):
            small = sum_ref[s][part(me2, 16), :]
            wait(two_in[s].at[pl.ds(0, 16 * (n2 - 1))], two_recv.at[s])
            for r in range(1, n2):
                small = small + two_in[s][part(lax.rem(me2 + r, n2), 16), :].astype(F32)
            three_ref[s][part(me3, 16), :] = small.astype(BF16)
            for r in range(1, n3):
                here = three_ref[s].at[part(me3, 16)]
                remote(here, here, three_recv.at[s],
                       at3(lax.rem(me3 + r, n3))).start()

    send_boundary(back_ref, ret_ref, 1, *BATCHES[3])

    def final(s, rows, count):
        first, width = strips[s][:2]
        return gw_ref.at[core, pl.ds(rows, count), pl.ds(first, width)]

    for s, (first, width, (n1, me1, _), (n2, me2, at2), (n3, _, _)) in enumerate(strips):
        with jax.named_scope("gather_one_%d" % s):
            wait(three_ref[s].at[pl.ds(0, 16 * (n3 - 1))], three_recv.at[s])
            done = three_ref[s][0:16, :].astype(F32)
            for i in range(1, n3):
                done = done + three_ref[s][16 * i:16 * i + 16, :].astype(F32)
            row = pl.multiple_of(me1 * (512 // n1) + me2 * 16, 16)
            gw_ref[core, pl.ds(row, 16), pl.ds(first, width)] = done.astype(BF16)
            for r in range(1, n2):
                remote(final(s, row, 16), final(s, row, 16), ag1_recv.at[s],
                       at2(lax.rem(me2 + r, n2))).start()

    send_boundary(back_ref, ret_ref, 1, *BATCHES[4])

    def forward(s, row, count):
        remote(final(s, row, count), final(s, row, count), fin_recv, sibling).start()

    units = []
    for s, (_, _, (n1, _, _), _, _) in enumerate(strips):
        units.append(units[-1] + (4 if strips[s - 1][2][0] == 4 else 1) if s else 0)

    for s in sorted(range(len(strips)), key=lambda s: strips[s][2][0] == 4):
        _, _, (n1, me1, at1), (n2, _, _), _ = strips[s]
        with jax.named_scope("gather_two_%d" % s):
            rows1 = 512 // n1
            wait(final(s, 0, 16 * (n2 - 1)), ag1_recv.at[s])
            row = pl.multiple_of(me1 * rows1, rows1)
            for r in range(1, n1):
                unit = units[s] + me1 if n1 == 4 else units[s]
                remote(final(s, row, rows1), final(s, row, rows1), ag2_recv.at[unit],
                       at1(lax.rem(me1 + r, n1))).start()
            if n1 == 4:
                forward(s, row, rows1)

    send_boundary(back_ref, ret_ref, 1, *BATCHES[5])

    with jax.named_scope("forward"):
        for s, (_, _, (n1, me1, _), _, _) in enumerate(strips):
            if n1 == 4:
                for r in range(1, 4):
                    i = lax.rem(me1 + r, 4)
                    row = pl.multiple_of(i * 128, 128)
                    wait(final(s, row, 128), ag2_recv.at[units[s] + i])
                    forward(s, row, 128)
            else:
                wait(final(s, 0, 448), ag2_recv.at[units[s]])
                forward(s, 0, 512)

    with jax.named_scope("wait_grads"):
        wait_boundary(ret_ref, 1)
    with jax.named_scope("feature_grads"):
        returned = dot(sel_ref[...], ret_ref[...])
        gfeat_ref[...] = (
            base_ref[...] + jnp.concatenate([returned[0:128], returned[128:256]], axis=1)
        ).astype(BF16)

    with jax.named_scope("finish"):
        wait(all_sent_ref, sent)
        wait(gw_ref.at[other], fin_recv)


def write_kernel(gfeat_in, gw_in, gfeat_ref, gws_ref, gwn_ref, wide_ref, sem):
    copies = [pltpu.make_async_copy(gfeat_in, gfeat_ref, sem.at[0])]
    copies[0].start()
    for c, ref in enumerate((gws_ref, gwn_ref)):
        for piece in range(4):
            rows = pl.ds(128 * piece, 128)
            wide_ref[c, rows, :] = gw_in[c, rows, :].astype(F32)
            copy = pltpu.make_async_copy(
                wide_ref.at[c, rows], ref.at[rows], sem.at[1 + 4 * c + piece])
            copy.start()
            copies.append(copy)
    for copy in copies:
        copy.wait()


def strip_scratch(shape, dtype):
    return tuple(
        pltpu.VMEM(shape(width, 4 if order[0] == "x" else 8), dtype) for _, width, order in STRIPS
    )


def sent_rows():
    length = {"x": 4, "y": 8, "z": 8}
    rows = 2 * 63 * 8 + 2 * 128 + 512
    for _, width, order in STRIPS:
        n1, n2, n3 = (length[axis] for axis in order)
        steps = 2 * (512 - 512 // n1) + 2 * 16 * (n2 - 1) + 16 * (n3 - 1)
        rows += steps * width // 512
    return rows


def local(features, w_self, w_neigh, cotangent, neighbors, send_rows, send_count):
    vmem = pl.BlockSpec(memory_space=pltpu.VMEM)
    hbm = pl.BlockSpec(memory_space=pltpu.HBM)
    dma = pltpu.SemaphoreType.DMA
    grad_features, grads = pl.pallas_call(
        kernel,
        out_shape=(
            pltpu.VMEM((128, 512), BF16),
            pltpu.VMEM((2, 512, 512), BF16),
        ),
        in_specs=[hbm] * 7,
        out_specs=(vmem, vmem),
        scratch_shapes=[
            pltpu.VMEM((128, 512), BF16),
            pltpu.VMEM((2, 512, 512), BF16),
            pltpu.VMEM((128, 512), BF16),
            pltpu.VMEM((16, 128), jnp.int32),
            pltpu.VMEM((8, 64), jnp.int32),
            pltpu.VMEM((1, 64), jnp.int32),
            pltpu.VMEM((256, 1024), BF16),
            pltpu.VMEM((256, 1024), BF16),
            pltpu.VMEM((1024, 256), BF16),
            pltpu.VMEM((1024, 256), BF16),
            pltpu.VMEM((1024, 256), BF16),
            pltpu.VMEM((1024, 256), BF16),
            pltpu.VMEM((1024, 256), BF16),
            pltpu.VMEM((2, 512, 128), BF16),
            pltpu.VMEM((512, 128), BF16),
            pltpu.VMEM((256, 512), BF16),
            pltpu.VMEM((512, 512), F32),
            strip_scratch(lambda w, n: (512, w), BF16),
            strip_scratch(lambda w, n: (512, w), BF16),
            strip_scratch(lambda w, n: (512 // n, w), F32),
            strip_scratch(lambda w, n: (512 // n, w), BF16),
            strip_scratch(lambda w, n: (512 // n, w), BF16),
            strip_scratch(lambda w, n: (128, w), BF16),
            pltpu.VMEM((128, 512), F32),
            pltpu.VMEM((sent_rows(), 512), BF16),
            dma((6,)), dma, dma((2,)), dma((2,)), *([dma((len(STRIPS),))] * 4),
            dma((sum(4 if order[0] == "x" else 1 for _, _, order in STRIPS),)), dma,
        ],
        compiler_params=pltpu.CompilerParams(
            collective_id=0, has_side_effects=True, vmem_limit_bytes=40 << 20
        ),
        name="sage_backward",
    )(*(
        pltpu.with_memory_space_constraint(array, pltpu.HBM)
        for array in (
            features, w_self, w_neigh, cotangent, neighbors.T,
            send_rows.reshape(64, 8).T, send_count.reshape(1, 64),
        )
    ))
    return pl.pallas_call(
        write_kernel,
        out_shape=(
            jax.ShapeDtypeStruct((128, 512), BF16),
            jax.ShapeDtypeStruct((512, 512), F32),
            jax.ShapeDtypeStruct((512, 512), F32),
        ),
        in_specs=[vmem, vmem],
        out_specs=(hbm, hbm, hbm),
        scratch_shapes=[pltpu.VMEM((2, 512, 512), F32), dma((9,))],
        compiler_params=pltpu.CompilerParams(vmem_limit_bytes=8 << 20),
        name="write_results",
    )(grad_features, grads)


def solution(mesh):
    placed = (
        P(("grp", "dom"), None),
        P(),
        P(),
        P(("grp", "dom"), None),
        P(("grp", "dom"), None),
        P("grp", "dom", None, None),
        P("grp", "dom", None),
    )
    return jax.shard_map(
        local,
        mesh=mesh,
        in_specs=placed,
        out_specs=(P(("grp", "dom"), None), P(), P()),
        check_vma=False,
    )
```
